256 devices in a mesh: seq: 128 (over x, z, y), vocab: 2 (over core).
Axes of the slice: x: 4, y: 4, z: 8, core: 2. Of those that a mesh axis runs over, the one named last changes fastest.
Arguments:
- mamba_in: bfloat16 [32768, 6144], P('seq', 'vocab'), may hold values from -6 to 6
- mamba_gate: bfloat16 [32768, 6144], P('seq', 'vocab'), may hold values from -6 to 6
- conv_weight: float32 [4, 6144], P(None, 'vocab'), may hold values from -0.6 to 0.6
- conv_bias: float32 [6144], P('vocab'), may hold values from -0.5 to 0.5
- x_proj: bfloat16 [6144, 224], P('vocab'), may hold values from -0.078125 to 0.078125
- dt_proj: bfloat16 [192, 6144], P(None, 'vocab'), may hold values from -0.4375 to 0.4375
- dt_bias: float32 [6144], P('vocab'), may hold values from -16 to -4
- a_log: float32 [16, 6144], P(None, 'vocab'), may hold values from 0 to 2.77
- d_skip: float32 [6144], P('vocab'), may hold values from 0.5 to 1.5
- queries: bfloat16 [32768, 3072], P('seq', 'vocab'), may hold values from -6 to 6
- keys: bfloat16 [32768, 384], P('seq', 'vocab'), may hold values from -6 to 6
- att_values: bfloat16 [32768, 384], P('seq', 'vocab'), may hold values from -6 to 6
- logits: bfloat16 [32768, 16384], P('seq', 'vocab'), may hold values from -260 to 260
- targets: int32 [32768], P('seq'), may hold values from 0 to 16383
- allowed: int32 [32768, 2048], P('seq', 'vocab'), may hold values from 0 to 255, as said below
Outputs:
- mamba_out: bfloat16 [32768, 6144], P('seq', 'vocab')
- attention_out: bfloat16 [32768, 3072], P('seq', 'vocab')
- loglik: float32 [32768], P('seq')
The draws below stay inside these ranges and needn't reach their ends.
Inputs may be any that keep to these rules, and one draw needn't show every extreme that they name: `allowed`: the bit of each token's target is set in its mask.
All inputs are finite; a program needn't handle non-finite values.
Results may differ from the reference program's by a relative error of at most 0.0027.
The reference program's roundings to bfloat16 on the way (of `conv_out`, `dt_low` and `weights`) count: a program that leaves them out, or rounds other values in their place, can miss the bound.
Values may be sent and summed in bfloat16 or wider, within the bound.
No kernel may reach another device: no remote copies, remote signals or barrier semaphores. Data moves between devices by JAX's collectives and lax.ppermute only.
A program may use at most 256 MiB of HBM per device.

```python
import math
import jax
import jax.numpy as jnp
from jax import lax

INNER = 6144
STATE = 16
RANK = 192
HEADS = 32
KV_HEADS = 4
HEAD_DIM = 96
WINDOW = 2048
VOCAB = 16384
KCONV = 4
TOK_DEV = 256
TOKENS = 32768


def attention_pair(key):
    base = jax.random.fold_in(key, 7)
    key_q, key_k = jax.random.split(base, 2)
    width_q = HEADS * HEAD_DIM
    width_k = KV_HEADS * HEAD_DIM
    query_arr = jnp.clip(jax.random.normal(key_q, (TOKENS, width_q), jnp.float32), -6.0, 6.0)
    key_arr = jnp.clip(jax.random.normal(key_k, (TOKENS, width_k), jnp.float32), -6.0, 6.0)
    return (query_arr, key_arr)


def draw_queries(key, part):
    return attention_pair(key)[0].astype(jnp.bfloat16)


def draw_keys(key, part):
    return attention_pair(key)[1].astype(jnp.bfloat16)


def target_ids(key):
    return jax.random.randint(jax.random.fold_in(key, 21), (TOKENS,), 0, VOCAB, dtype=jnp.int32)


def draw_targets(key, part):
    return target_ids(key)


def draw_allowed(key, part):
    wanted = target_ids(key)
    words = jax.random.randint(jax.random.fold_in(key, 22), (TOKENS, VOCAB // 8), 0, 256, dtype=jnp.int32)
    one = jnp.int32(1)
    target_bit = jnp.left_shift(one, wanted % 8)
    partner_bit = jnp.left_shift(one, jnp.bitwise_xor(wanted, 1) % 8)
    word_ids = jnp.arange(VOCAB // 8, dtype=jnp.int32)
    forced = jnp.where(word_ids[None, :] == (wanted // 8)[:, None], jnp.bitwise_or(target_bit, partner_bit)[:, None], jnp.int32(0))
    result = jnp.bitwise_or(words, forced)
    row_ids = jnp.arange(TOKENS, dtype=jnp.int32)
    other_word = (wanted // 8 + 1) % (VOCAB // 8)
    at_other = word_ids[None, :] == other_word[:, None]
    result = jnp.where(at_other & (row_ids[:, None] == 0), jnp.int32(0), result)
    result = jnp.where(at_other & (row_ids[:, None] == 1), jnp.int32(255), result)
    return result


def draw_logits(key, part):
    key_b = jax.random.fold_in(jax.random.fold_in(key, 23), 0)
    base = jnp.clip(3.0 * jax.random.normal(key_b, (TOKENS, VOCAB), jnp.float32), -18.0, 18.0)
    return base.astype(jnp.bfloat16)


def levels(key, dims, cuts, smallest, high):
    def one(position, blocks):
        heights = jax.random.uniform(jax.random.fold_in(jax.random.fold_in(key, 6), position), (blocks,), jnp.float32, smallest / len(cuts), high / len(cuts))
        return jnp.repeat(jnp.exp(heights), dims[position] // blocks).reshape((-1,) + (1,) * (len(dims) - position - 1))

    level = one(*cuts[0])
    for cut in cuts[1:]:
        level = level * one(*cut)
    return level


def centred(rng, extent, width, bound, shards=(), kind=jnp.bfloat16):
    entries = jax.random.normal(rng, extent, jnp.float32) * width
    if len(shards) > 0:
        entries = levels(rng, extent, shards, -0.22, 0.18) * entries
    return jnp.clip(entries, min=-bound, max=bound).astype(kind)


def setup_inputs(seed: int = 0) -> dict:
    arg_keys = jax.random.split(jax.random.key(seed), 16)
    return {
        "mamba_in": centred(arg_keys[0], (TOKENS, INNER), 1.0, 6.0, ((0, 128), (1, 2))),
        "mamba_gate": centred(arg_keys[1], (TOKENS, INNER), 1.0, 6.0, ((0, 128), (1, 2))),
        "conv_weight": jnp.clip(jax.random.uniform(arg_keys[2], (KCONV, INNER), jnp.float32, -0.6, 0.6) * levels(arg_keys[2], (KCONV, INNER), ((1, 2),), -0.4, 0.0), -0.6, 0.6),
        "conv_bias": jnp.clip(jax.random.uniform(arg_keys[3], (INNER,), jnp.float32, -0.5, 0.5) * levels(arg_keys[3], (INNER,), ((0, 2),), -0.4, 0.0), -0.5, 0.5),
        "x_proj": centred(arg_keys[4], (INNER, RANK + 2 * STATE), INNER ** -0.5, 0.078125, ((0, 2),)),
        "dt_proj": centred(arg_keys[5], (RANK, INNER), RANK ** -0.5, 0.4375, ((1, 2),)),
        "dt_bias": jnp.clip(-16.0 + 12.0 * jax.random.uniform(arg_keys[6], (INNER,), jnp.float32) ** levels(arg_keys[6], (INNER,), ((0, 2),), -0.2, 0.2), -16.0, -4.0),
        "a_log": jnp.clip(2.77 * jax.random.uniform(arg_keys[7], (STATE, INNER), jnp.float32) ** levels(arg_keys[7], (STATE, INNER), ((1, 2),), -0.2, 0.2), 0.0, 2.77),
        "d_skip": jnp.clip(1.0 + 0.1 * jax.random.normal(arg_keys[8], (INNER,), jnp.float32), 0.5, 1.5),
        "queries": draw_queries(jax.random.fold_in(arg_keys[15], 71), 0),
        "keys": draw_keys(jax.random.fold_in(arg_keys[15], 71), 0),
        "att_values": centred(arg_keys[11], (TOKENS, KV_HEADS * HEAD_DIM), 1.0, 6.0, ((0, 128), (1, 2))),
        "logits": draw_logits(jax.random.fold_in(arg_keys[15], 71), 0),
        "targets": draw_targets(jax.random.fold_in(arg_keys[15], 71), 0),
        "allowed": draw_allowed(jax.random.fold_in(arg_keys[15], 71), 0),
    }


def mamba_part(mamba_in, mamba_gate, conv_weight, conv_bias, x_proj, dt_proj, dt_bias, a_log, d_skip):
    source = mamba_in.astype(jnp.float32)
    padded = jnp.concatenate((jnp.zeros((KCONV - 1, INNER), jnp.float32), source), axis=0)
    conv = conv_bias[None, :] + jnp.zeros((TOKENS, INNER), jnp.float32)
    for tap in range(KCONV):
        conv = conv + conv_weight[tap][None, :] * padded[tap:tap + TOKENS]
    conv_out = jax.nn.silu(conv).astype(jnp.bfloat16)
    proj = jnp.dot(conv_out, x_proj, preferred_element_type=jnp.float32)
    dt_low = proj[:, :RANK].astype(jnp.bfloat16)
    b_all = proj[:, RANK:RANK + STATE]
    c_all = proj[:, RANK + STATE:]
    a_mat = -jnp.exp(a_log)
    inputs_f = conv_out.astype(jnp.float32)
    block = math.gcd(TOKENS, 64)

    def token_step(state, inputs):
        delta_t, input_t, b_t, c_t = inputs
        state = jnp.exp(delta_t[None, :] * a_mat) * state + (delta_t * input_t)[None, :] * b_t[:, None]
        return state, jnp.sum(c_t[:, None] * state, axis=0)

    def block_step(state, index):
        start = (index * block).astype(jnp.int32)
        low_rows = lax.dynamic_slice_in_dim(dt_low, start, block, 0)
        delta = jax.nn.softplus(jnp.dot(low_rows, dt_proj, preferred_element_type=jnp.float32) + dt_bias[None, :])
        rows_in = lax.dynamic_slice_in_dim(inputs_f, start, block, 0)
        rows_b = lax.dynamic_slice_in_dim(b_all, start, block, 0)
        rows_c = lax.dynamic_slice_in_dim(c_all, start, block, 0)
        return lax.scan(token_step, state, (delta, rows_in, rows_b, rows_c))

    _, outputs = lax.scan(block_step, jnp.zeros((STATE, INNER), jnp.float32), jnp.arange(TOKENS // block, dtype=jnp.int32))
    result = outputs.reshape(TOKENS, INNER) + d_skip[None, :] * inputs_f
    return (result * jax.nn.silu(mamba_gate.astype(jnp.float32))).astype(jnp.bfloat16)


def attention_part(queries, keys, att_values):
    groups = HEADS // KV_HEADS
    scale = HEAD_DIM ** -0.5
    query_all = queries.reshape(TOKENS, KV_HEADS, groups, HEAD_DIM)
    key_pad = jnp.concatenate((jnp.zeros((WINDOW, KV_HEADS * HEAD_DIM), jnp.bfloat16), keys), axis=0).reshape(WINDOW + TOKENS, KV_HEADS, HEAD_DIM)
    value_pad = jnp.concatenate((jnp.zeros((WINDOW, KV_HEADS * HEAD_DIM), jnp.bfloat16), att_values), axis=0).reshape(WINDOW + TOKENS, KV_HEADS, HEAD_DIM)
    span = WINDOW + TOK_DEV

    def one_block(index):
        start = (index * TOK_DEV).astype(jnp.int32)
        query_rows = lax.dynamic_slice_in_dim(query_all, start, TOK_DEV, 0).astype(jnp.float32)
        key_rows = lax.dynamic_slice_in_dim(key_pad, start, span, 0).astype(jnp.float32)
        value_rows = lax.dynamic_slice_in_dim(value_pad, start, span, 0).astype(jnp.float32)
        score = jnp.einsum('qkgd,ckd->kgqc', query_rows, key_rows) * scale
        qpos = jnp.arange(TOK_DEV, dtype=jnp.int32)[:, None]
        cpos = jnp.arange(span, dtype=jnp.int32)[None, :]
        visible = (cpos > qpos) & (cpos <= WINDOW + qpos) & (start - WINDOW + cpos >= 0)
        score = jnp.where(visible[None, None], score, -jnp.inf)
        top = jnp.max(score, axis=3, keepdims=True)
        prob = jnp.exp(score - top)
        total = jnp.sum(prob, axis=3)
        weights = lax.optimization_barrier(prob.astype(jnp.bfloat16)).astype(jnp.float32)
        mixed = jnp.einsum('kgqc,ckd->qkgd', weights, value_rows)
        mixed = mixed / jnp.transpose(total, (2, 0, 1))[:, :, :, None]
        return mixed.reshape(TOK_DEV, HEADS * HEAD_DIM).astype(jnp.bfloat16)

    blocks = lax.map(one_block, jnp.arange(TOKENS // TOK_DEV, dtype=jnp.int32))
    return blocks.reshape(TOKENS, HEADS * HEAD_DIM)


def scoring_part(logits, targets, allowed):
    def one_block(index):
        start = (index * TOK_DEV).astype(jnp.int32)
        rows = lax.dynamic_slice_in_dim(logits, start, TOK_DEV, 0).astype(jnp.float32)
        words = lax.dynamic_slice_in_dim(allowed, start, TOK_DEV, 0)
        wanted = lax.dynamic_slice_in_dim(targets, start, TOK_DEV, 0)
        bits = (jnp.right_shift(words[:, :, None], jnp.arange(8, dtype=jnp.int32)[None, None, :]) & 1).reshape(TOK_DEV, VOCAB) == 1
        masked = jnp.where(bits, rows, -jnp.inf)
        top = jnp.max(masked, axis=1)
        total = jnp.sum(jnp.exp(masked - top[:, None]), axis=1)
        target_logit = jnp.take_along_axis(rows, wanted[:, None].astype(jnp.int32), axis=1)[:, 0]
        return target_logit - top - jnp.log(total)

    return lax.map(one_block, jnp.arange(TOKENS // TOK_DEV, dtype=jnp.int32)).reshape(TOKENS)


def reference(mamba_in, mamba_gate, conv_weight, conv_bias, x_proj, dt_proj, dt_bias, a_log, d_skip, queries, keys, att_values, logits, targets, allowed):
    mamba_out = mamba_part(mamba_in, mamba_gate, conv_weight, conv_bias, x_proj, dt_proj, dt_bias, a_log, d_skip)
    attention_out = attention_part(queries, keys, att_values)
    loglik = scoring_part(logits, targets, allowed)
    return (mamba_out, attention_out, loglik)
```

```python
import jax
import jax.numpy as jnp
from jax import lax
from jax.experimental import pallas as pl
from jax.experimental.pallas import tpu as pltpu
from jax.sharding import PartitionSpec as P

HEADS = 32
KV_HEADS = 4
HEAD_DIM = 96
WINDOW = 2048
LOG2E = 1.4426950408889634
F32 = jnp.float32
BF16 = jnp.bfloat16
GROUP = 1024
LANES = 128
LOW = -1e30


def params(mib):
    return pltpu.CompilerParams(vmem_limit_bytes=mib * 1024 * 1024)


def cost(flops, nbytes, trans=0):
    return pl.CostEstimate(flops=int(flops), bytes_accessed=int(nbytes), transcendentals=int(trans))


def shifted(value, axis, steps):
    count = lax.axis_size(axis)
    leading, last = (max(0, -steps), min(count, count - steps))
    return lax.ppermute(value, axis, [(source, source + steps) for source in range(leading, last)])


def swapped(value):
    return lax.ppermute(value, "vocab", [(0, 1), (1, 0)])


def score_kernel(logits_ref, allowed_ref, local_target_ref, out_ref):
    rows, width = logits_ref.shape
    words = LANES
    span = words * 8
    row_id = lax.broadcasted_iota(jnp.int32, (words, span), 0)
    col_id = lax.broadcasted_iota(jnp.int32, (words, span), 1)
    expand = jnp.where(row_id == col_id // 8, 1.0, 0.0).astype(BF16)
    col = lax.broadcasted_iota(jnp.int32, (rows, span), 1)
    bit = jnp.left_shift(jnp.int32(1), col & 7)
    wanted = local_target_ref[...]
    top = jnp.full((rows, LANES), -jnp.inf, F32)
    target = jnp.zeros((rows, LANES), F32)
    parts = []
    for block in range(width // span):
        values = logits_ref[:, block * span : (block + 1) * span].astype(F32)
        word = allowed_ref[:, block * words : (block + 1) * words].astype(F32).astype(BF16)
        spread = jnp.dot(word, expand, preferred_element_type=F32).astype(jnp.int32)
        masked = jnp.where((spread & bit) != 0, values, -jnp.inf)
        hit = jnp.where(col == wanted - block * span, values, 0.0)
        for piece in range(8):
            at = slice(piece * LANES, (piece + 1) * LANES)
            top = jnp.maximum(top, masked[:, at])
            target = target + hit[:, at]
        parts.append(masked)
    best = jnp.maximum(jnp.max(top, axis=1, keepdims=True), LOW)
    total = jnp.zeros((rows, LANES), F32)
    for masked in parts:
        terms = jnp.exp(masked - best)
        for piece in range(8):
            total = total + terms[:, piece * LANES : (piece + 1) * LANES]
    summed = jnp.sum(total, axis=1, keepdims=True)
    found = jnp.sum(target, axis=1, keepdims=True)
    lane = lax.broadcasted_iota(jnp.int32, (rows, LANES), 1)
    out_ref[...] = jnp.where(lane == 0, best, jnp.where(lane == 1, summed, found))


def scoring_part(logits, targets, allowed):
    rows, width = logits.shape
    block = 32
    local_target = (targets - lax.axis_index("vocab") * width).reshape(rows, 1)
    stats = pl.pallas_call(
        score_kernel,
        grid=(rows // block,),
        in_specs=[
            pl.BlockSpec((block, width), lambda i: (i, 0)),
            pl.BlockSpec((block, width // 8), lambda i: (i, 0)),
            pl.BlockSpec((block, 1), lambda i: (i, 0)),
        ],
        out_specs=pl.BlockSpec((block, LANES), lambda i: (i, 0)),
        out_shape=jax.ShapeDtypeStruct((rows, LANES), F32),
        compiler_params=params(48),
        cost_estimate=cost(rows * width * 256, rows * width * 3, rows * width),
        name="scoring",
    )(logits, allowed, local_target)
    return stats[:, :8].T


def scoring_join(mine, other):
    top = jnp.maximum(mine[0], other[0])
    total = mine[1] * jnp.exp(mine[0] - top) + other[1] * jnp.exp(other[0] - top)
    return mine[2] + other[2] - top - jnp.log(total)


def conv_kernel(x_ref, rim_ref, weight_ref, bias_ref, proj_ref, conv_ref, out_ref, pad):
    rows = x_ref.shape[0]
    taps = weight_ref.shape[0]
    x = x_ref[...].astype(F32)
    pad[8 : 8 + rows, :] = x
    pad[8 - (taps - 1) : 8, :] = rim_ref[...].astype(F32)
    conv = bias_ref[...]
    for tap in range(taps):
        start = 8 - (taps - 1) + tap
        conv = conv + weight_ref[tap : tap + 1, :] * pad[start : start + rows, :]
    value = (conv / (1.0 + jnp.exp(-conv))).astype(BF16)
    conv_ref[...] = value
    part = jnp.dot(value, proj_ref[...], preferred_element_type=F32)

    @pl.when(pl.program_id(0) == 0)
    def _():
        out_ref[...] = part

    @pl.when(pl.program_id(0) > 0)
    def _():
        out_ref[...] += part


def convolve(mamba_in, rim, conv_weight, conv_bias, x_proj):
    rows, channels = mamba_in.shape
    taps = conv_weight.shape[0]
    width = x_proj.shape[1]
    block = 512
    return pl.pallas_call(
        conv_kernel,
        grid=(channels // block,),
        in_specs=[
            pl.BlockSpec((rows, block), lambda i: (0, i)),
            pl.BlockSpec((taps - 1, block), lambda i: (0, i)),
            pl.BlockSpec((taps, block), lambda i: (0, i)),
            pl.BlockSpec((1, block), lambda i: (0, i)),
            pl.BlockSpec((block, width), lambda i: (i, 0)),
        ],
        out_specs=[
            pl.BlockSpec((rows, block), lambda i: (0, i)),
            pl.BlockSpec((rows, width), lambda i: (0, 0)),
        ],
        out_shape=[
            jax.ShapeDtypeStruct((rows, channels), BF16),
            jax.ShapeDtypeStruct((rows, width), F32),
        ],
        scratch_shapes=[pltpu.VMEM((rows + 8, block), F32)],
        compiler_params=params(32),
        cost_estimate=cost(rows * channels * 700, rows * channels * 4, rows * channels * 2),
        name="convolution",
    )(mamba_in, rim, conv_weight, conv_bias.reshape(1, channels), x_proj)


def softplus(v):
    e = jnp.exp(-jnp.abs(v))
    return jnp.maximum(v, 0.0) + jnp.log1p(e)


def scan_kernel(
    low_ref, dt_ref, bias_ref, alog_ref, skip_ref, conv_ref, b_ref, c_ref,
    y_ref, cum_ref, end_ref, delta_s, x_s,
):
    rows = low_ref.shape[0]
    nstate = alog_ref.shape[0]
    delta = softplus(jnp.dot(low_ref[...], dt_ref[...], preferred_element_type=F32) + bias_ref[...])
    x = conv_ref[...].astype(F32)
    for sub in range(8):
        at = slice(sub * LANES, (sub + 1) * LANES)
        delta_s[:, sub, :] = delta[:, at]
        x_s[:, sub, :] = x[:, at]
    rate = [-LOG2E * jnp.exp(alog_ref[n]) for n in range(nstate)]
    skip = skip_ref[...]

    def step(t, carry):
        cum, state = carry
        d = delta_s[t]
        x_t = x_s[t]
        cum = cum + d
        dx = d * x_t
        y = skip * x_t
        new = []
        for n in range(nstate):
            row = t * nstate + n
            h = jnp.exp2(d * rate[n]) * state[n] + dx * b_ref[pl.ds(row, 1), :]
            y = y + h * c_ref[pl.ds(row, 1), :]
            new.append(h)
        cum_ref[t] = cum
        y_ref[t] = y
        return cum, tuple(new)

    zero = jnp.zeros((8, LANES), F32)
    _, state = lax.fori_loop(0, rows, step, (zero, (zero,) * nstate), unroll=4)
    for n in range(nstate):
        end_ref[n] = state[n]


def local_scan(dt_low, dt_proj, dt_bias, a_log, d_skip, conv_out, b_wide, c_wide):
    rows, channels = conv_out.shape
    rank = dt_low.shape[1]
    nstate = a_log.shape[0]
    subs = channels // LANES
    wide = pl.BlockSpec((rows * nstate, LANES), lambda i: (0, 0))
    folded = pl.BlockSpec((rows, 8, LANES), lambda i: (0, i, 0))
    states = pl.BlockSpec((nstate, 8, LANES), lambda i: (0, i, 0))
    return pl.pallas_call(
        scan_kernel,
        grid=(channels // GROUP,),
        in_specs=[
            pl.BlockSpec((rows, rank), lambda i: (0, 0)),
            pl.BlockSpec((rank, GROUP), lambda i: (0, i)),
            pl.BlockSpec((1, GROUP), lambda i: (0, i)),
            states,
            pl.BlockSpec((8, LANES), lambda i: (i, 0)),
            pl.BlockSpec((rows, GROUP), lambda i: (0, i)),
            wide,
            wide,
        ],
        out_specs=[folded, folded, states],
        out_shape=[
            jax.ShapeDtypeStruct((rows, subs, LANES), F32),
            jax.ShapeDtypeStruct((rows, subs, LANES), F32),
            jax.ShapeDtypeStruct((nstate, subs, LANES), F32),
        ],
        scratch_shapes=[pltpu.VMEM((rows, 8, LANES), F32), pltpu.VMEM((rows, 8, LANES), F32)],
        compiler_params=params(48),
        cost_estimate=cost(rows * channels * nstate * 500, rows * channels * 12, rows * channels * nstate),
        name="local_scan",
    )(
        dt_low, dt_proj, dt_bias.reshape(1, channels), a_log, d_skip.reshape(subs, LANES),
        conv_out, b_wide, c_wide,
    )


def finish_kernel(y_ref, cum_ref, c_ref, state_ref, alog_ref, gate_ref, out_ref, y_s):
    rows = y_ref.shape[0]
    nstate = alog_ref.shape[0]
    rate = [-LOG2E * jnp.exp(alog_ref[n]) for n in range(nstate)]
    state = [state_ref[n] for n in range(nstate)]

    def step(t, carry):
        cum = cum_ref[t]
        y = y_ref[t]
        for n in range(nstate):
            y = y + (jnp.exp2(cum * rate[n]) * state[n]) * c_ref[pl.ds(t * nstate + n, 1), :]
        y_s[t] = y
        return carry

    lax.fori_loop(0, rows, step, 0, unroll=4)
    for sub in range(8):
        at = slice(sub * LANES, (sub + 1) * LANES)
        gate = gate_ref[:, at].astype(F32)
        out_ref[:, at] = (y_s[:, sub, :] * (gate / (1.0 + jnp.exp(-gate)))).astype(BF16)


def finish(y, cum, c_wide, incoming, a_log, mamba_gate):
    rows, channels = mamba_gate.shape
    nstate = a_log.shape[0]
    folded = pl.BlockSpec((rows, 8, LANES), lambda i: (0, i, 0))
    states = pl.BlockSpec((nstate, 8, LANES), lambda i: (0, i, 0))
    return pl.pallas_call(
        finish_kernel,
        grid=(channels // GROUP,),
        in_specs=[
            folded,
            folded,
            pl.BlockSpec((rows * nstate, LANES), lambda i: (0, 0)),
            states,
            states,
            pl.BlockSpec((rows, GROUP), lambda i: (0, i)),
        ],
        out_specs=pl.BlockSpec((rows, GROUP), lambda i: (0, i)),
        out_shape=jax.ShapeDtypeStruct((rows, channels), BF16),
        scratch_shapes=[pltpu.VMEM((rows, 8, LANES), F32)],
        compiler_params=params(48),
        cost_estimate=cost(rows * channels * nstate * 300, rows * channels * 12, rows * channels * nstate),
        name="finish",
    )(y, cum, c_wide, incoming, a_log, mamba_gate)


def entering(summed, state, rate):
    nstate = state.shape[0]
    place = lax.axis_index("seq")
    count = lax.axis_size("seq")

    def join(earlier, later):
        return (earlier[0] + later[0], earlier[1] * jnp.exp(rate * later[0][None]) + later[1])

    def packed(pair):
        high = pair[0].astype(BF16)
        low = (pair[0] - high.astype(F32)).astype(BF16)
        return jnp.concatenate((pair[1].astype(BF16), high[None], low[None]), axis=0)

    def opened(message):
        wide = message.astype(F32)
        return (wide[nstate] + wide[nstate + 1], wide[:nstate])

    total = (summed, state)
    before = None
    stride = 1
    for size in (4, 2, 4, 4):
        message = packed(total)
        mine = (place // stride) % size
        came = [message]
        for k in range(1, size):
            pairs = [(i, i ^ (k * stride)) for i in range(count)]
            came.append(lax.ppermute(message, "seq", pairs))
        ordered = []
        for j in range(size):
            pick = mine ^ j
            chosen = came[0]
            for k in range(1, size):
                chosen = jnp.where(pick == k, came[k], chosen)
            ordered.append(opened(chosen))
        prefix = (jnp.zeros_like(summed), jnp.zeros_like(state))
        running = None
        for j in range(size):
            running = ordered[j] if running is None else join(running, ordered[j])
            if j < size - 1:
                prefix = tuple(jnp.where(mine == j + 1, r, p) for r, p in zip(running, prefix))
        before = prefix if before is None else join(prefix, before)
        total = running
        stride *= size
    return before[1]


def attention_kernel(first_ref, turn_ref, q_ref, own_ref, z1_ref, z2_ref, r1_ref, r2_ref, r3_ref,
                     out_ref, key_s, value_s, query_s, mixed_s, score_s):
    rows = own_ref.shape[0]
    local_kv = own_ref.shape[1] // (2 * HEAD_DIM)
    groups = HEADS // KV_HEADS
    tiles = WINDOW // rows + 1
    first = first_ref[0]
    turn = turn_ref[0]
    lane = lax.broadcasted_iota(jnp.int32, (rows, LANES - HEAD_DIM), 1)
    one = jnp.where(lane == 0, 1.0, 0.0).astype(BF16)
    moved = (None, r1_ref, r2_ref, r3_ref)
    for tile in range(tiles):
        if tile % 4 == 0:
            block = (z2_ref, z1_ref, own_ref)[tile // 4][...]
        else:
            step = 4 - tile % 4
            early = tile < 4
            part = jnp.where((turn < step) == early, 1, 0)
            block = moved[step][part]
        closed = jnp.where(tile < first, LOW, 0.0)
        extra = jnp.where(lane == 0, closed, 0.0).astype(BF16)
        for head in range(local_kv):
            key = block[:, head * HEAD_DIM : (head + 1) * HEAD_DIM]
            value = block[:, (local_kv + head) * HEAD_DIM : (local_kv + head + 1) * HEAD_DIM]
            key_s[head, tile * rows : (tile + 1) * rows, :] = jnp.concatenate((key, extra), axis=1)
            value_s[head, tile * rows : (tile + 1) * rows, :] = jnp.concatenate((value, one), axis=1)
    for head in range(local_kv * groups):
        query = q_ref[:, head * HEAD_DIM : (head + 1) * HEAD_DIM]
        query_s[head] = jnp.concatenate((query, one), axis=1)
    qpos = lax.broadcasted_iota(jnp.int32, (rows, rows), 0)
    cpos = lax.broadcasted_iota(jnp.int32, (rows, rows), 1)
    factor = HEAD_DIM ** (-0.5) * LOG2E

    for kv in range(local_kv):

        def one_head(index, carry):
            head = kv * groups + index
            query = query_s[head]
            top = jnp.full((rows, LANES), -jnp.inf, F32)
            for tile in range(tiles):
                key = key_s[kv, tile * rows : (tile + 1) * rows, :]
                score = lax.dot_general(query, key, (((1,), (1,)), ((), ())), preferred_element_type=F32)
                if tile == 0:
                    score = jnp.where(cpos > qpos, score, -jnp.inf)
                if tile == tiles - 1:
                    score = jnp.where(cpos <= qpos, score, -jnp.inf)
                score_s[:, tile * rows : (tile + 1) * rows] = score
                for piece in range(rows // LANES):
                    top = jnp.maximum(top, score[:, piece * LANES : (piece + 1) * LANES])
            best = jnp.max(top, axis=1, keepdims=True)
            total = jnp.zeros((rows, LANES), F32)
            mixed = jnp.zeros((rows, LANES), F32)
            for tile in range(tiles):
                prob = jnp.exp2((score_s[:, tile * rows : (tile + 1) * rows] - best) * factor)
                for piece in range(rows // LANES):
                    total = total + prob[:, piece * LANES : (piece + 1) * LANES]
                value = value_s[kv, tile * rows : (tile + 1) * rows, :]
                mixed = mixed + jnp.dot(prob.astype(BF16), value, preferred_element_type=F32)
            mixed_s[head] = (mixed / jnp.sum(total, axis=1, keepdims=True)).astype(BF16)
            return carry

        lax.fori_loop(0, groups, one_head, 0)
    for head in range(local_kv * groups):
        out_ref[:, head * HEAD_DIM : (head + 1) * HEAD_DIM] = mixed_s[head][:, :HEAD_DIM]


def attention_part(queries, keys, att_values):
    rows = queries.shape[0]
    count = lax.axis_size("seq")
    place = lax.axis_index("seq")
    turn = place % 4
    local_heads = queries.shape[1] // HEAD_DIM
    local_kv = keys.shape[1] // HEAD_DIM
    tiles = WINDOW // rows + 1
    own = jnp.concatenate((keys, att_values), axis=1)
    z1 = shifted(own, "seq", 4)
    z2 = shifted(own, "seq", 8)
    moved = []
    for step in (1, 2, 3):
        payload = jnp.stack((z1, jnp.where(turn + step >= 4, z2, own)))
        pairs = [(i, i - i % 4 + (i + step) % 4) for i in range(count)]
        moved.append(lax.ppermute(payload, "seq", pairs))
    first = jnp.maximum(tiles - 1 - place, 0).astype(jnp.int32).reshape(1)
    smem = pl.BlockSpec(memory_space=pltpu.SMEM)
    vmem = pl.BlockSpec(memory_space=pltpu.VMEM)
    pairs = rows * rows * tiles * local_heads
    return pl.pallas_call(
        attention_kernel,
        in_specs=[smem, smem] + [vmem] * 7,
        out_specs=vmem,
        out_shape=jax.ShapeDtypeStruct(queries.shape, BF16),
        scratch_shapes=[
            pltpu.VMEM((local_kv, tiles * rows, LANES), BF16),
            pltpu.VMEM((local_kv, tiles * rows, LANES), BF16),
            pltpu.VMEM((local_heads, rows, LANES), BF16),
            pltpu.VMEM((local_heads, rows, LANES), BF16),
            pltpu.VMEM((rows, tiles * rows), F32),
        ],
        compiler_params=params(48),
        cost_estimate=cost(pairs * 1200, rows * 4096 * 3, pairs),
        name="attention",
    )(first, turn.astype(jnp.int32).reshape(1), queries, own, z1, z2, *moved)


def local(
    mamba_in, mamba_gate, conv_weight, conv_bias, x_proj, dt_proj, dt_bias, a_log, d_skip,
    queries, keys, att_values, logits, targets, allowed,
):
    rows, channels = mamba_in.shape
    taps = conv_weight.shape[0]
    rank = dt_proj.shape[0]
    nstate = a_log.shape[0]
    subs = channels // LANES
    rim = shifted(mamba_in[rows - (taps - 1) :], "seq", 1)
    stats = scoring_part(logits, targets, allowed)
    conv_out, part = convolve(mamba_in, rim, conv_weight, conv_bias, x_proj)
    proj = part + swapped(part)
    dt_low = proj[:, :rank].astype(BF16)
    b_wide = jnp.broadcast_to(proj[:, rank : rank + nstate].reshape(rows * nstate, 1), (rows * nstate, LANES))
    c_wide = jnp.broadcast_to(proj[:, rank + nstate :].reshape(rows * nstate, 1), (rows * nstate, LANES))
    folded = a_log.reshape(nstate, subs, LANES)
    y, cum, end = local_scan(dt_low, dt_proj, dt_bias, folded, d_skip, conv_out, b_wide, c_wide)
    incoming = entering(cum[rows - 1], end, -jnp.exp(folded))
    attention_out = attention_part(queries, keys, att_values)
    loglik = scoring_join(stats, swapped(stats))
    mamba_out = finish(y, cum, c_wide, incoming, folded, mamba_gate)
    return (mamba_out, attention_out, loglik)


def solution(mesh):
    in_specs = (
        P("seq", "vocab"),
        P("seq", "vocab"),
        P(None, "vocab"),
        P("vocab"),
        P("vocab", None),
        P(None, "vocab"),
        P("vocab"),
        P(None, "vocab"),
        P("vocab"),
        P("seq", "vocab"),
        P("seq", "vocab"),
        P("seq", "vocab"),
        P("seq", "vocab"),
        P("seq"),
        P("seq", "vocab"),
    )
    out_specs = (P("seq", "vocab"), P("seq", "vocab"), P("seq"))
    return jax.shard_map(local, mesh=mesh, in_specs=in_specs, out_specs=out_specs, check_vma=False)
```

```python
import functools

import jax
import jax.numpy as jnp
from jax import lax
from jax.experimental import pallas as pl
from jax.experimental.pallas import tpu as pltpu
from jax.sharding import PartitionSpec as P

HEADS = 32
KV_HEADS = 4
HEAD_DIM = 96
WINDOW = 2048
LOG2E = 1.4426950408889634
F32 = jnp.float32
BF16 = jnp.bfloat16
GROUP = 1024
LANES = 128
LOW = -1e30
PIECES = 4
TOKENS = 16


def params(mib):
    return pltpu.CompilerParams(vmem_limit_bytes=mib * 1024 * 1024)


def cost(flops, nbytes, trans=0):
    return pl.CostEstimate(flops=int(flops), bytes_accessed=int(nbytes), transcendentals=int(trans))


def shifted(value, axis, steps):
    count = lax.axis_size(axis)
    leading, last = (max(0, -steps), min(count, count - steps))
    return lax.ppermute(value, axis, [(source, source + steps) for source in range(leading, last)])


def swapped(value):
    return lax.ppermute(value, "vocab", [(0, 1), (1, 0)])


def score_kernel(logits_ref, allowed_ref, local_target_ref, *refs):
    out_ref = refs[-1]
    rows, width = logits_ref.shape
    words = LANES
    span = words * 8
    row_id = lax.broadcasted_iota(jnp.int32, (words, span), 0)
    col_id = lax.broadcasted_iota(jnp.int32, (words, span), 1)
    expand = jnp.where(row_id == col_id // 8, 1.0, 0.0).astype(BF16)
    col = lax.broadcasted_iota(jnp.int32, (rows, span), 1)
    bit = jnp.left_shift(jnp.int32(1), col & 7)
    wanted = local_target_ref[...]
    top = jnp.full((rows, LANES), -jnp.inf, F32)
    target = jnp.zeros((rows, LANES), F32)
    parts = []
    for block in range(width // span):
        values = logits_ref[:, block * span : (block + 1) * span].astype(F32)
        word = allowed_ref[:, block * words : (block + 1) * words].astype(F32).astype(BF16)
        spread = jnp.dot(word, expand, preferred_element_type=F32).astype(jnp.int32)
        masked = jnp.where((spread & bit) != 0, values, -jnp.inf)
        hit = jnp.where(col == wanted - block * span, values, 0.0)
        for piece in range(8):
            at = slice(piece * LANES, (piece + 1) * LANES)
            top = jnp.maximum(top, masked[:, at])
            target = target + hit[:, at]
        parts.append(masked)
    best = jnp.maximum(jnp.max(top, axis=1, keepdims=True), LOW)
    total = jnp.zeros((rows, LANES), F32)
    for masked in parts:
        terms = jnp.exp(masked - best)
        for piece in range(8):
            total = total + terms[:, piece * LANES : (piece + 1) * LANES]
    summed = jnp.sum(total, axis=1, keepdims=True)
    found = jnp.sum(target, axis=1, keepdims=True)
    lane = lax.broadcasted_iota(jnp.int32, (rows, LANES), 1)
    out_ref[...] = jnp.where(lane == 0, best, jnp.where(lane == 1, summed, found))


def scoring_part(logits, targets, allowed, after):
    rows, width = logits.shape
    block = 32
    local_target = (targets - lax.axis_index("vocab") * width).reshape(rows, 1)
    stats = pl.pallas_call(
        score_kernel,
        grid=(rows // block,),
        in_specs=[
            pl.BlockSpec((block, width), lambda i: (i, 0)),
            pl.BlockSpec((block, width // 8), lambda i: (i, 0)),
            pl.BlockSpec((block, 1), lambda i: (i, 0)),
        ]
        + [pl.BlockSpec(memory_space=pl.ANY)] * len(after),
        out_specs=pl.BlockSpec((block, LANES), lambda i: (i, 0)),
        out_shape=jax.ShapeDtypeStruct((rows, LANES), F32),
        compiler_params=params(48),
        cost_estimate=cost(rows * width * 256, rows * width * 3, rows * width),
        name="scoring",
    )(logits, allowed, local_target, *after)
    return stats[:, :8].T


def scoring_join(mine, other):
    top = jnp.maximum(mine[0], other[0])
    total = mine[1] * jnp.exp(mine[0] - top) + other[1] * jnp.exp(other[0] - top)
    return mine[2] + other[2] - top - jnp.log(total)


def conv_kernel(x_ref, rim_ref, weight_ref, bias_ref, proj_ref, conv_ref, out_ref, pad):
    rows = x_ref.shape[0]
    taps = weight_ref.shape[0]
    x = x_ref[...].astype(F32)
    pad[8 : 8 + rows, :] = x
    pad[8 - (taps - 1) : 8, :] = rim_ref[...].astype(F32)
    conv = bias_ref[...]
    for tap in range(taps):
        start = 8 - (taps - 1) + tap
        conv = conv + weight_ref[tap : tap + 1, :] * pad[start : start + rows, :]
    value = (conv / (1.0 + jnp.exp(-conv))).astype(BF16)
    conv_ref[...] = value
    part = lax.dot_general(value, proj_ref[...], (((1,), (1,)), ((), ())), preferred_element_type=F32)

    @pl.when(pl.program_id(0) == 0)
    def _():
        out_ref[...] = part

    @pl.when(pl.program_id(0) > 0)
    def _():
        out_ref[...] += part


def convolve(mamba_in, rim, conv_weight, conv_bias, x_proj):
    rows, channels = mamba_in.shape
    taps = conv_weight.shape[0]
    width = x_proj.shape[0]
    block = 1024
    return pl.pallas_call(
        conv_kernel,
        grid=(channels // block,),
        in_specs=[
            pl.BlockSpec((rows, block), lambda i: (0, i)),
            pl.BlockSpec((taps - 1, block), lambda i: (0, i)),
            pl.BlockSpec((taps, block), lambda i: (0, i)),
            pl.BlockSpec((1, block), lambda i: (0, i)),
            pl.BlockSpec((width, block), lambda i: (0, i)),
        ],
        out_specs=[
            pl.BlockSpec((rows, block), lambda i: (0, i)),
            pl.BlockSpec((rows, width), lambda i: (0, 0)),
        ],
        out_shape=[
            jax.ShapeDtypeStruct((rows, channels), BF16),
            jax.ShapeDtypeStruct((rows, width), F32),
        ],
        scratch_shapes=[pltpu.VMEM((rows + 8, block), F32)],
        compiler_params=params(60),
        cost_estimate=cost(rows * channels * 700, rows * channels * 4, rows * channels * 2),
        name="convolution",
    )(mamba_in, rim, conv_weight, conv_bias.reshape(1, channels), x_proj)


def softplus(v):
    e = jnp.exp(-jnp.abs(v))
    return jnp.maximum(v, 0.0) + jnp.log1p(e)


def spread(table, wide_s, rows):
    for n in range(table.shape[1]):
        wide_s[n * rows : (n + 1) * rows, :] = jnp.broadcast_to(table[:, n : n + 1], (rows, LANES))


def scan_kernel(
    mine_ref, other_ref, dt_ref, bias_ref, alog_ref, skip_ref, conv_ref, after_ref,
    y_ref, cum_ref, message_ref, delta_s, x_s, wide_s, rate_s,
):
    rows, rank = mine_ref.shape[0], dt_ref.shape[0]
    nstate = alog_ref.shape[0]

    @pl.when(pl.program_id(0) == 0)
    def _():
        spread(mine_ref[:, rank:] + other_ref[:, rank:], wide_s, rows)

    low = (mine_ref[:, :rank] + other_ref[:, :rank]).astype(BF16)
    for sub in range(8):
        at = slice(sub * LANES, (sub + 1) * LANES)
        product = jnp.dot(low, dt_ref[:, at], preferred_element_type=F32)
        delta_s[:, sub, :] = softplus(product + bias_ref[:, at])
        x_s[:, sub, :] = conv_ref[:, at].astype(F32)
    for n in range(nstate):
        rate_s[n] = -LOG2E * jnp.exp(alog_ref[n])

    def step(block, carry):
        cum, state = carry
        start = block * TOKENS
        ds = [delta_s[start + k] for k in range(TOKENS)]
        xs = [x_s[start + k] for k in range(TOKENS)]
        cums, ys = [], []
        for k in range(TOKENS):
            cum = cum + ds[k]
            dx = ds[k] * xs[k]
            sums = [skip_ref[...] * xs[k], jnp.zeros_like(cum)]
            new = []
            for n in range(nstate):
                row = n * rows + start + k
                h = jnp.exp2(ds[k] * rate_s[n]) * state[n] + dx * wide_s[pl.ds(row, 1), :]
                sums[n % 2] = sums[n % 2] + h * wide_s[pl.ds(row + nstate * rows, 1), :]
                new.append(h)
            state = tuple(new)
            cums.append(cum)
            ys.append(sums[0] + sums[1])
        for k in range(TOKENS):
            cum_ref[start + k] = cums[k]
            y_ref[start + k] = ys[k]
        return cum, state

    zero = jnp.zeros((8, LANES), F32)
    cum, state = lax.fori_loop(0, rows // TOKENS, step, (zero, (zero,) * nstate))
    high = cum.astype(BF16).astype(F32)
    message_ref[0] = jnp.concatenate(state + (high, cum - high), axis=0).astype(BF16)


def local_scan(mine, other, dt_proj, dt_bias, a_log, d_skip, conv_out, after):
    rows, channels = conv_out.shape
    rank = dt_proj.shape[0]
    nstate = a_log.shape[0]
    subs = channels // LANES
    folded = pl.BlockSpec((rows, 8, LANES), lambda i: (0, i, 0))
    states = pl.BlockSpec((nstate, 8, LANES), lambda i: (0, i, 0))
    whole = pl.BlockSpec(mine.shape, lambda i: (0, 0))
    return pl.pallas_call(
        scan_kernel,
        grid=(channels // GROUP,),
        in_specs=[
            whole,
            whole,
            pl.BlockSpec((rank, GROUP), lambda i: (0, i)),
            pl.BlockSpec((1, GROUP), lambda i: (0, i)),
            states,
            pl.BlockSpec((8, LANES), lambda i: (i, 0)),
            pl.BlockSpec((rows, GROUP), lambda i: (0, i)),
            pl.BlockSpec(memory_space=pl.ANY),
        ],
        out_specs=[folded, folded, pl.BlockSpec((1, 8 * (nstate + 2), LANES), lambda i: (i, 0, 0))],
        out_shape=[
            jax.ShapeDtypeStruct((rows, subs, LANES), F32),
            jax.ShapeDtypeStruct((rows, subs, LANES), F32),
            jax.ShapeDtypeStruct((channels // GROUP, 8 * (nstate + 2), LANES), BF16),
        ],
        scratch_shapes=[
            pltpu.VMEM((rows, 8, LANES), F32),
            pltpu.VMEM((rows, 8, LANES), F32),
            pltpu.VMEM((rows * nstate * 2, LANES), F32),
            pltpu.VMEM((nstate, 8, LANES), F32),
        ],
        compiler_params=params(62),
        cost_estimate=cost(rows * channels * nstate * 1600, rows * channels * 12, rows * channels * nstate),
        name="local_scan",
    )(
        mine, other, dt_proj, dt_bias.reshape(1, channels), a_log, d_skip.reshape(subs, LANES),
        conv_out, after,
    )


def finish_kernel(y_ref, cum_ref, mine_ref, other_ref, state_ref, alog_ref, gate_ref, out_ref, y_s, wide_s, rate_s):
    rows = y_ref.shape[0]
    nstate = alog_ref.shape[0]
    start = mine_ref.shape[1] - nstate

    @pl.when(pl.program_id(0) == 0)
    def _():
        spread(mine_ref[:, start:] + other_ref[:, start:], wide_s, rows)

    for n in range(nstate):
        rate_s[n] = -LOG2E * jnp.exp(alog_ref[n])

    def step(block, carry):
        start = block * TOKENS
        cums = [cum_ref[start + k] for k in range(TOKENS)]
        ys = [[y_ref[start + k], jnp.zeros((8, LANES), F32)] for k in range(TOKENS)]
        for n in range(nstate):
            rate, state = rate_s[n], state_ref[0, 8 * n : 8 * n + 8, :]
            for k in range(TOKENS):
                term = (jnp.exp2(cums[k] * rate) * state) * wide_s[pl.ds(n * rows + start + k, 1), :]
                ys[k][n % 2] = ys[k][n % 2] + term
        for k in range(TOKENS):
            y_s[start + k] = ys[k][0] + ys[k][1]
        return carry

    lax.fori_loop(0, rows // TOKENS, step, 0)
    for sub in range(8):
        at = slice(sub * LANES, (sub + 1) * LANES)
        half = 0.5 * gate_ref[:, at].astype(F32)
        out_ref[:, at] = (y_s[:, sub, :] * (half * jnp.tanh(half) + half)).astype(BF16)


def finish(y, cum, mine, other, incoming, a_log, mamba_gate):
    rows, channels = mamba_gate.shape
    nstate = a_log.shape[0]
    folded = pl.BlockSpec((rows, 8, LANES), lambda i: (0, i, 0))
    states = pl.BlockSpec((nstate, 8, LANES), lambda i: (0, i, 0))
    whole = pl.BlockSpec(mine.shape, lambda i: (0, 0))
    return pl.pallas_call(
        finish_kernel,
        grid=(channels // GROUP,),
        in_specs=[
            folded,
            folded,
            whole,
            whole,
            pl.BlockSpec((1, 8 * nstate, LANES), lambda i: (i, 0, 0)),
            states,
            pl.BlockSpec((rows, GROUP), lambda i: (0, i)),
        ],
        out_specs=pl.BlockSpec((rows, GROUP), lambda i: (0, i)),
        out_shape=jax.ShapeDtypeStruct((rows, channels), BF16),
        scratch_shapes=[
            pltpu.VMEM((rows, 8, LANES), F32),
            pltpu.VMEM((rows * nstate, LANES), F32),
            pltpu.VMEM((nstate, 8, LANES), F32),
        ],
        compiler_params=params(48),
        cost_estimate=cost(rows * channels * nstate * 1000, rows * channels * 12, rows * channels * nstate),
        name="finish",
    )(y, cum, mine, other, incoming, a_log, mamba_gate)


def join_kernel(size, first, last, place_ref, alog_ref, *refs):
    came, refs = refs[:size], refs[size:]
    if not first:
        old_sum_ref, old_ref, refs = refs[0], refs[1], refs[2:]
    nstate = alog_ref.shape[0]
    mine = place_ref[0]
    groups = came[0].shape[0]
    for g in range(groups):
        at = slice(8 * g, 8 * g + 8)
        ordered = []
        for j in range(size):
            pick = mine ^ j
            chosen = came[0][g]
            for k in range(1, size):
                chosen = jnp.where(pick == k, came[k][g], chosen)
            ordered.append(chosen.astype(F32))
        row = lambda j, n: ordered[j][8 * n : 8 * n + 8, :]
        added = [row(j, nstate) + row(j, nstate + 1) for j in range(size)]
        zero = jnp.zeros((8, LANES), F32)
        running, prefix = added[0], zero
        for j in range(1, size):
            prefix = jnp.where(mine == j, running, prefix)
            running = running + added[j]
        total_rows = []
        for n in range(nstate):
            rate = -LOG2E * jnp.exp(alog_ref[n, at, :])
            state, before = row(0, n), zero
            for j in range(1, size):
                before = jnp.where(mine == j, state, before)
                if j < size - 1 or not last:
                    state = state * jnp.exp2(rate * added[j]) + row(j, n)
            if not first:
                before = before * jnp.exp2(rate * old_sum_ref[g]) + old_ref[g, 8 * n : 8 * n + 8, :]
            refs[0][g, 8 * n : 8 * n + 8, :] = before
            total_rows.append(state)
        if not last:
            refs[1][g] = prefix if first else prefix + old_sum_ref[g]
            high = running.astype(BF16).astype(F32)
            refs[2][g] = jnp.concatenate(total_rows + [high, running - high], axis=0).astype(BF16)


def joined(message, a_log, beside):
    nstate = a_log.shape[0]
    groups = message.shape[0]
    place = lax.axis_index("seq")
    count = lax.axis_size("seq")
    smem = pl.BlockSpec(memory_space=pltpu.SMEM)
    vmem = pl.BlockSpec(memory_space=pltpu.VMEM)
    stride = 1
    old = []
    results = []
    sizes = (4, 2, 4, 4)
    for stage, (size, work) in enumerate(zip(sizes, beside)):
        first, last = stage == 0, stage == len(sizes) - 1
        mine = ((place // stride) % size).astype(jnp.int32).reshape(1)
        came = [message]
        for k in range(1, size):
            pairs = [(i, i ^ (k * stride)) for i in range(count)]
            came.append(lax.ppermute(message, "seq", pairs))
        done = [piece(message) for piece in work]
        if done:
            came, done = lax.optimization_barrier((came, done))
        results.extend(done)
        shapes = [jax.ShapeDtypeStruct((groups, 8 * nstate, LANES), F32)]
        if not last:
            shapes += [jax.ShapeDtypeStruct((groups, 8, LANES), F32), jax.ShapeDtypeStruct(message.shape, BF16)]
        outs = pl.pallas_call(
            functools.partial(join_kernel, size, first, last),
            in_specs=[smem] + [vmem] * (1 + size + len(old)),
            out_specs=[vmem] * len(shapes),
            out_shape=shapes,
            compiler_params=params(24),
            cost_estimate=cost(1e8, message.size * 2 * size, message.size * size),
            name="join",
        )(mine, a_log, *came, *old)
        if not last:
            old = [outs[1], outs[0]]
            message = outs[2]
        stride *= size
    return outs[0], results


def payload_kernel(turn_ref, own_ref, z1_ref, z2_ref, *outs):
    for step, out_ref in enumerate(outs, 1):
        out_ref[0] = z1_ref[...]
        wraps = turn_ref[0] + step >= 4

        @pl.when(wraps)
        def _():
            out_ref[1] = z2_ref[...]

        @pl.when(jnp.logical_not(wraps))
        def _():
            out_ref[1] = own_ref[...]


def payloads(turn, own, z1, z2):
    smem = pl.BlockSpec(memory_space=pltpu.SMEM)
    vmem = pl.BlockSpec(memory_space=pltpu.VMEM)
    return pl.pallas_call(
        payload_kernel,
        in_specs=[smem, vmem, vmem, vmem],
        out_specs=[vmem] * 3,
        out_shape=[jax.ShapeDtypeStruct((2,) + own.shape, BF16)] * 3,
        compiler_params=params(32),
        cost_estimate=cost(0, own.size * 18, 0),
        name="payload",
    )(turn, own, z1, z2)


def prepare_kernel(first_ref, turn_ref, own_ref, z1_ref, z2_ref, r1_ref, r2_ref, r3_ref, key_ref, value_ref):
    rows = own_ref.shape[1]
    local_kv = own_ref.shape[0] // (2 * HEAD_DIM)
    tiles = WINDOW // rows + 1
    first = first_ref[0]
    turn = turn_ref[0]
    pad = LANES - HEAD_DIM
    line = lax.broadcasted_iota(jnp.int32, (pad, rows), 0)
    empty = jnp.zeros((rows, pad), BF16)
    moved = (None, r1_ref, r2_ref, r3_ref)
    for tile in range(tiles):
        at = slice(tile * rows, (tile + 1) * rows)
        if tile % 4 == 0:
            block = (z2_ref, z1_ref, own_ref)[tile // 4][...]
        else:
            step = 4 - tile % 4
            early = tile < 4
            block = moved[step][jnp.where((turn < step) == early, 1, 0)]
        extra = jnp.where(line == 0, jnp.where(tile < first, LOW, 0.0), 0.0).astype(BF16)
        for head in range(local_kv):
            key = block[head * HEAD_DIM : (head + 1) * HEAD_DIM, :]
            value = block[(local_kv + head) * HEAD_DIM : (local_kv + head + 1) * HEAD_DIM, :]
            key_ref[head, :, at] = jnp.concatenate((key, extra), axis=0)
            turned = jnp.transpose(value.astype(F32)).astype(BF16)
            value_ref[head, at, :] = jnp.concatenate((turned, empty), axis=1)


def prepare(first, turn, own, z1, z2, moved):
    rows = own.shape[1]
    local_kv = own.shape[0] // (2 * HEAD_DIM)
    span = WINDOW + rows
    smem = pl.BlockSpec(memory_space=pltpu.SMEM)
    vmem = pl.BlockSpec(memory_space=pltpu.VMEM)
    return pl.pallas_call(
        prepare_kernel,
        in_specs=[smem, smem] + [vmem] * 6,
        out_specs=[vmem, vmem],
        out_shape=[
            jax.ShapeDtypeStruct((local_kv, LANES, span), BF16),
            jax.ShapeDtypeStruct((local_kv, span, LANES), BF16),
        ],
        compiler_params=params(32),
        cost_estimate=cost(1e9, own.size * 18, 0),
        name="prepare",
    )(first, turn, own, z1, z2, *moved)


def attention_kernel(q_ref, key_ref, value_ref, after_ref, out_ref, score_a, score_b):
    rows, width = q_ref.shape
    span = key_ref.shape[2]
    tiles = span // rows
    heads = width // HEAD_DIM
    lane = lax.broadcasted_iota(jnp.int32, (rows, LANES - HEAD_DIM), 1)
    one = jnp.where(lane == 0, 1.0, 0.0).astype(BF16)
    qpos = lax.broadcasted_iota(jnp.int32, (rows, rows), 0)
    cpos = lax.broadcasted_iota(jnp.int32, (rows, rows), 1)
    factor = HEAD_DIM ** (-0.5) * LOG2E
    store = (score_a, score_b)

    def query_of(head):
        return jnp.concatenate((q_ref[:, head * HEAD_DIM : (head + 1) * HEAD_DIM], one), axis=1)

    def scored(query, head, tile, top):
        at = slice(tile * rows, (tile + 1) * rows)
        score = jnp.dot(query, key_ref[0, :, at], preferred_element_type=F32)
        if tile == 0:
            score = jnp.where(cpos > qpos, score, -jnp.inf)
        if tile == tiles - 1:
            score = jnp.where(cpos <= qpos, score, -jnp.inf)
        store[head % 2][:, at] = score
        for piece in range(rows // LANES):
            top = jnp.maximum(top, score[:, piece * LANES : (piece + 1) * LANES])
        return top

    low = jnp.full((rows, LANES), -jnp.inf, F32)
    top = low
    query = query_of(0)
    for tile in range(tiles):
        top = scored(query, 0, tile, top)
    for head in range(heads):
        best = jnp.max(top, axis=1, keepdims=True)
        total = jnp.zeros((rows, LANES), F32)
        mixed = jnp.zeros((rows, LANES), F32)
        top = low
        if head + 1 < heads:
            query = query_of(head + 1)
        for tile in range(tiles):
            at = slice(tile * rows, (tile + 1) * rows)
            if head + 1 < heads:
                top = scored(query, head + 1, tile, top)
            prob = jnp.exp2((store[head % 2][:, at] - best) * factor)
            for piece in range(rows // LANES):
                total = total + prob[:, piece * LANES : (piece + 1) * LANES]
            mixed = mixed + jnp.dot(prob.astype(BF16), value_ref[0, at, :], preferred_element_type=F32)
        result = mixed / jnp.sum(total, axis=1, keepdims=True)
        out_ref[:, head * HEAD_DIM : (head + 1) * HEAD_DIM] = result[:, :HEAD_DIM].astype(BF16)


def attention_piece(queries, key, value, piece, after):
    rows = queries.shape[0]
    local_kv, _, span = key.shape
    heads = queries.shape[1] // HEAD_DIM
    share = heads // PIECES
    kv = piece * share // (heads // local_kv)
    pairs = rows * span * share
    return pl.pallas_call(
        attention_kernel,
        grid=(1,),
        in_specs=[
            pl.BlockSpec((rows, share * HEAD_DIM), lambda i: (0, piece)),
            pl.BlockSpec((1, LANES, span), lambda i: (kv, 0, 0)),
            pl.BlockSpec((1, span, LANES), lambda i: (kv, 0, 0)),
            pl.BlockSpec(memory_space=pl.ANY),
        ],
        out_specs=pl.BlockSpec((rows, share * HEAD_DIM), lambda i: (0, 0)),
        out_shape=jax.ShapeDtypeStruct((rows, share * HEAD_DIM), BF16),
        scratch_shapes=[pltpu.VMEM((rows, span), F32), pltpu.VMEM((rows, span), F32)],
        compiler_params=params(48),
        cost_estimate=cost(pairs * 2600, rows * 4096, pairs),
        name="attention",
    )(queries, key, value, after)


def local(
    mamba_in, mamba_gate, conv_weight, conv_bias, x_proj, dt_proj, dt_bias, a_log, d_skip,
    queries, keys, att_values, logits, targets, allowed,
):
    rows, channels = mamba_in.shape
    taps = conv_weight.shape[0]
    nstate = a_log.shape[0]
    subs = channels // LANES
    place = lax.axis_index("seq")
    count = lax.axis_size("seq")
    rim = shifted(mamba_in[rows - (taps - 1) :], "seq", 1)
    own = jnp.concatenate((keys.T, att_values.T), axis=0)
    z1 = shifted(own, "seq", 4)
    z2 = shifted(own, "seq", 8)
    first = jnp.maximum(WINDOW // rows - place, 0).astype(jnp.int32).reshape(1)
    turn = (place % 4).astype(jnp.int32).reshape(1)
    sent = payloads(turn, own, z1, z2)
    moved = []
    for step, payload in enumerate(sent, 1):
        pairs = [(i, i - i % 4 + (i + step) % 4) for i in range(count)]
        moved.append(lax.ppermute(payload, "seq", pairs))
    conv_out, part = convolve(mamba_in, rim, conv_weight, conv_bias, x_proj.T)
    other = swapped(part)
    folded = a_log.reshape(nstate, subs, LANES)
    y, cum, message = local_scan(part, other, dt_proj, dt_bias, folded, d_skip, conv_out, sent[2])
    made = {}

    def score(message):
        return scoring_part(logits, targets, allowed, [message] + moved)

    def attend(piece):
        def run(message):
            if not made:
                made["kv"] = prepare(first, turn, own, z1, z2, moved)
            return attention_piece(queries, *made["kv"], piece, message)

        return run

    incoming, results = joined(message, folded, [[score], [attend(0)], [attend(1), attend(2)], [attend(3)]])
    stats = results[0]
    attention_out = jnp.concatenate(results[1:], axis=1)
    loglik = scoring_join(stats, swapped(stats))
    mamba_out = finish(y, cum, part, other, incoming, folded, mamba_gate)
    return (mamba_out, attention_out, loglik)


def solution(mesh):
    in_specs = (
        P("seq", "vocab"),
        P("seq", "vocab"),
        P(None, "vocab"),
        P("vocab"),
        P("vocab", None),
        P(None, "vocab"),
        P("vocab"),
        P(None, "vocab"),
        P("vocab"),
        P("seq", "vocab"),
        P("seq", "vocab"),
        P("seq", "vocab"),
        P("seq", "vocab"),
        P("seq"),
        P("seq", "vocab"),
    )
    out_specs = (P("seq", "vocab"), P("seq", "vocab"), P("seq"))
    return jax.shard_map(local, mesh=mesh, in_specs=in_specs, out_specs=out_specs, check_vma=False)
```

```python
import functools

import jax
import jax.numpy as jnp
from jax import lax
from jax.experimental import pallas as pl
from jax.experimental.pallas import tpu as pltpu
from jax.sharding import PartitionSpec as P

HEADS = 32
KV_HEADS = 4
HEAD_DIM = 96
WINDOW = 2048
LOG2E = 1.4426950408889634
F32 = jnp.float32
BF16 = jnp.bfloat16
GROUP = 1024
LANES = 128
LOW = -1e30
PIECES = 4
TOKENS = 16


def params(mib):
    return pltpu.CompilerParams(vmem_limit_bytes=mib * 1024 * 1024)


def cost(flops, nbytes, trans=0):
    return pl.CostEstimate(flops=int(flops), bytes_accessed=int(nbytes), transcendentals=int(trans))


def shifted(value, axis, steps):
    count = lax.axis_size(axis)
    leading, last = (max(0, -steps), min(count, count - steps))
    return lax.ppermute(value, axis, [(source, source + steps) for source in range(leading, last)])


def swapped(value):
    return lax.ppermute(value, "vocab", [(0, 1), (1, 0)])


def score_kernel(logits_ref, allowed_ref, local_target_ref, *refs):
    out_ref = refs[-1]
    rows, width = logits_ref.shape
    words = LANES
    span = words * 8
    row_id = lax.broadcasted_iota(jnp.int32, (words, span), 0)
    col_id = lax.broadcasted_iota(jnp.int32, (words, span), 1)
    expand = jnp.where(row_id == col_id // 8, 1.0, 0.0).astype(BF16)
    col = lax.broadcasted_iota(jnp.int32, (rows, span), 1)
    bit = jnp.left_shift(jnp.int32(1), col & 7)
    wanted = local_target_ref[...]
    top = jnp.full((rows, LANES), -jnp.inf, F32)
    target = jnp.zeros((rows, LANES), F32)
    parts = []
    for block in range(width // span):
        values = logits_ref[:, block * span : (block + 1) * span].astype(F32)
        word = allowed_ref[:, block * words : (block + 1) * words].astype(F32).astype(BF16)
        spread = jnp.dot(word, expand, preferred_element_type=F32).astype(jnp.int32)
        masked = jnp.where((spread & bit) != 0, values, -jnp.inf)
        hit = jnp.where(col == wanted - block * span, values, 0.0)
        for piece in range(8):
            at = slice(piece * LANES, (piece + 1) * LANES)
            top = jnp.maximum(top, masked[:, at])
            target = target + hit[:, at]
        parts.append(masked)
    best = jnp.maximum(jnp.max(top, axis=1, keepdims=True), LOW)
    total = jnp.zeros((rows, LANES), F32)
    for masked in parts:
        terms = jnp.exp(masked - best)
        for piece in range(8):
            total = total + terms[:, piece * LANES : (piece + 1) * LANES]
    summed = jnp.sum(total, axis=1, keepdims=True)
    found = jnp.sum(target, axis=1, keepdims=True)
    lane = lax.broadcasted_iota(jnp.int32, (rows, LANES), 1)
    out_ref[...] = jnp.where(lane == 0, best, jnp.where(lane == 1, summed, found))


def scoring_part(logits, targets, allowed, after):
    rows, width = logits.shape
    block = 64
    local_target = (targets - lax.axis_index("vocab") * width).reshape(rows, 1)
    stats = pl.pallas_call(
        score_kernel,
        grid=(rows // block,),
        in_specs=[
            pl.BlockSpec((block, width), lambda i: (i, 0)),
            pl.BlockSpec((block, width // 8), lambda i: (i, 0)),
            pl.BlockSpec((block, 1), lambda i: (i, 0)),
        ]
        + [pl.BlockSpec(memory_space=pl.ANY)] * len(after),
        out_specs=pl.BlockSpec((block, LANES), lambda i: (i, 0)),
        out_shape=jax.ShapeDtypeStruct((rows, LANES), F32),
        compiler_params=params(24),
        cost_estimate=cost(rows * width * 256, rows * width * 3, rows * width),
        name="scoring",
    )(logits, allowed, local_target, *after)
    return stats[:, :8].T


def scoring_join(mine, other):
    top = jnp.maximum(mine[0], other[0])
    total = mine[1] * jnp.exp(mine[0] - top) + other[1] * jnp.exp(other[0] - top)
    return mine[2] + other[2] - top - jnp.log(total)


def conv_kernel(x_ref, rim_ref, weight_ref, bias_ref, proj_ref, conv_ref, out_ref, pad):
    rows = x_ref.shape[0]
    taps = weight_ref.shape[0]
    x = x_ref[...].astype(F32)
    pad[8 : 8 + rows, :] = x
    pad[8 - (taps - 1) : 8, :] = rim_ref[...].astype(F32)
    conv = bias_ref[...]
    for tap in range(taps):
        start = 8 - (taps - 1) + tap
        conv = conv + weight_ref[tap : tap + 1, :] * pad[start : start + rows, :]
    value = (conv / (1.0 + jnp.exp(-conv))).astype(BF16)
    conv_ref[...] = value
    part = lax.dot_general(value, proj_ref[...], (((1,), (1,)), ((), ())), preferred_element_type=F32)

    @pl.when(pl.program_id(0) == 0)
    def _():
        out_ref[...] = part

    @pl.when(pl.program_id(0) > 0)
    def _():
        out_ref[...] += part


def convolve(mamba_in, rim, conv_weight, conv_bias, x_proj):
    rows, channels = mamba_in.shape
    taps = conv_weight.shape[0]
    width = x_proj.shape[0]
    block = 1024
    return pl.pallas_call(
        conv_kernel,
        grid=(channels // block,),
        in_specs=[
            pl.BlockSpec((rows, block), lambda i: (0, i)),
            pl.BlockSpec((taps - 1, block), lambda i: (0, i)),
            pl.BlockSpec((taps, block), lambda i: (0, i)),
            pl.BlockSpec((1, block), lambda i: (0, i)),
            pl.BlockSpec((width, block), lambda i: (0, i)),
        ],
        out_specs=[
            pl.BlockSpec((rows, block), lambda i: (0, i)),
            pl.BlockSpec((rows, width), lambda i: (0, 0)),
        ],
        out_shape=[
            jax.ShapeDtypeStruct((rows, channels), BF16),
            jax.ShapeDtypeStruct((rows, width), F32),
        ],
        scratch_shapes=[pltpu.VMEM((rows + 8, block), F32)],
        compiler_params=params(60),
        cost_estimate=cost(rows * channels * 700, rows * channels * 4, rows * channels * 2),
        name="convolution",
    )(mamba_in, rim, conv_weight, conv_bias.reshape(1, channels), x_proj)


def softplus(v):
    e = jnp.exp(-jnp.abs(v))
    return jnp.maximum(v, 0.0) + jnp.log1p(e)


def spread(table, wide_s, rows):
    for n in range(table.shape[1]):
        wide_s[n * rows : (n + 1) * rows, :] = jnp.broadcast_to(table[:, n : n + 1], (rows, LANES))


def fold_rates(alog_ref, rate_s, group):
    for sub in range(8):
        at = slice(group * GROUP + sub * LANES, group * GROUP + (sub + 1) * LANES)
        rate_s[:, sub, :] = -LOG2E * jnp.exp(alog_ref[:, at])


def scan_kernel(
    mine_ref, other_ref, dt_ref, bias_ref, alog_ref, skip_ref, conv_ref, after_ref,
    y_ref, cum_ref, message_ref, delta_s, x_s, wide_s, rate_s,
):
    rows, rank = mine_ref.shape[0], dt_ref.shape[0]
    nstate = alog_ref.shape[0]
    spread(mine_ref[:, rank:] + other_ref[:, rank:], wide_s, rows)
    low = (mine_ref[:, :rank] + other_ref[:, :rank]).astype(BF16)
    for group in range(conv_ref.shape[1] // GROUP):
        here = slice(8 * group, 8 * group + 8)
        for sub in range(8):
            at = slice(group * GROUP + sub * LANES, group * GROUP + (sub + 1) * LANES)
            product = jnp.dot(low, dt_ref[:, at], preferred_element_type=F32)
            delta_s[:, sub, :] = softplus(product + bias_ref[:, at])
            x_s[:, sub, :] = conv_ref[:, at].astype(F32)
        fold_rates(alog_ref, rate_s, group)

        def step(block, carry):
            cum, state = carry
            start = block * TOKENS
            ds = [delta_s[start + k] for k in range(TOKENS)]
            xs = [x_s[start + k] for k in range(TOKENS)]
            cums, ys = [], []
            for k in range(TOKENS):
                cum = cum + ds[k]
                dx = ds[k] * xs[k]
                sums = [skip_ref[here, :] * xs[k], jnp.zeros_like(cum)]
                new = []
                for n in range(nstate):
                    row = n * rows + start + k
                    h = jnp.exp2(ds[k] * rate_s[n]) * state[n] + dx * wide_s[pl.ds(row, 1), :]
                    sums[n % 2] = sums[n % 2] + h * wide_s[pl.ds(row + nstate * rows, 1), :]
                    new.append(h)
                state = tuple(new)
                cums.append(cum)
                ys.append(sums[0] + sums[1])
            for k in range(TOKENS):
                cum_ref[start + k, here, :] = cums[k]
                y_ref[start + k, here, :] = ys[k]
            return cum, state

        zero = jnp.zeros((8, LANES), F32)
        cum, state = lax.fori_loop(0, rows // TOKENS, step, (zero, (zero,) * nstate))
        high = cum.astype(BF16).astype(F32)
        message_ref[group] = jnp.concatenate(state + (high, cum - high), axis=0).astype(BF16)


def local_scan(mine, other, dt_proj, dt_bias, a_log, d_skip, conv_out, after):
    rows, channels = conv_out.shape
    nstate = a_log.shape[0]
    subs = channels // LANES
    vmem = pl.BlockSpec(memory_space=pltpu.VMEM)
    return pl.pallas_call(
        scan_kernel,
        in_specs=[vmem] * 7 + [pl.BlockSpec(memory_space=pl.ANY)],
        out_specs=[vmem] * 3,
        out_shape=[
            jax.ShapeDtypeStruct((rows, subs, LANES), F32),
            jax.ShapeDtypeStruct((rows, subs, LANES), F32),
            jax.ShapeDtypeStruct((channels // GROUP, 8 * (nstate + 2), LANES), BF16),
        ],
        scratch_shapes=[
            pltpu.VMEM((rows, 8, LANES), F32),
            pltpu.VMEM((rows, 8, LANES), F32),
            pltpu.VMEM((rows * nstate * 2, LANES), F32),
            pltpu.VMEM((nstate, 8, LANES), F32),
        ],
        compiler_params=params(24),
        cost_estimate=cost(rows * channels * nstate * 1600, rows * channels * 12, rows * channels * nstate),
        name="local_scan",
    )(
        mine, other, dt_proj, dt_bias.reshape(1, channels), a_log, d_skip.reshape(subs, LANES),
        conv_out, after,
    )


def finish_kernel(y_ref, cum_ref, mine_ref, other_ref, state_ref, alog_ref, gate_ref, out_ref, y_s, wide_s, rate_s):
    rows = y_ref.shape[0]
    nstate = alog_ref.shape[0]
    spot = mine_ref.shape[1] - nstate
    spread(mine_ref[:, spot:] + other_ref[:, spot:], wide_s, rows)
    for group in range(gate_ref.shape[1] // GROUP):
        here = slice(8 * group, 8 * group + 8)
        fold_rates(alog_ref, rate_s, group)

        def step(block, carry):
            start = block * TOKENS
            cums = [cum_ref[start + k, here, :] for k in range(TOKENS)]
            ys = [[y_ref[start + k, here, :], jnp.zeros((8, LANES), F32)] for k in range(TOKENS)]
            for n in range(nstate):
                rate, state = rate_s[n], state_ref[group, 8 * n : 8 * n + 8, :]
                for k in range(TOKENS):
                    term = (jnp.exp2(cums[k] * rate) * state) * wide_s[pl.ds(n * rows + start + k, 1), :]
                    ys[k][n % 2] = ys[k][n % 2] + term
            for k in range(TOKENS):
                y_s[start + k] = ys[k][0] + ys[k][1]
            return carry

        lax.fori_loop(0, rows // TOKENS, step, 0)
        for sub in range(8):
            at = slice(group * GROUP + sub * LANES, group * GROUP + (sub + 1) * LANES)
            half = 0.5 * gate_ref[:, at].astype(F32)
            out_ref[:, at] = (y_s[:, sub, :] * (half * jnp.tanh(half) + half)).astype(BF16)


def finish(y, cum, mine, other, incoming, a_log, mamba_gate):
    rows, channels = mamba_gate.shape
    nstate = a_log.shape[0]
    vmem = pl.BlockSpec(memory_space=pltpu.VMEM)
    return pl.pallas_call(
        finish_kernel,
        in_specs=[vmem] * 7,
        out_specs=vmem,
        out_shape=jax.ShapeDtypeStruct((rows, channels), BF16),
        scratch_shapes=[
            pltpu.VMEM((rows, 8, LANES), F32),
            pltpu.VMEM((rows * nstate, LANES), F32),
            pltpu.VMEM((nstate, 8, LANES), F32),
        ],
        compiler_params=params(24),
        cost_estimate=cost(rows * channels * nstate * 1000, rows * channels * 12, rows * channels * nstate),
        name="finish",
    )(y, cum, mine, other, incoming, a_log, mamba_gate)


def join_kernel(size, first, last, place_ref, alog_ref, *refs):
    came, rate_s, refs = refs[:size], refs[-1], refs[size:-1]
    if not first:
        old_sum_ref, old_ref, refs = refs[0], refs[1], refs[2:]
    nstate = alog_ref.shape[0]
    mine = place_ref[0]
    groups = came[0].shape[0]
    for g in range(groups):
        fold_rates(alog_ref, rate_s, g)
        ordered = []
        for j in range(size):
            pick = mine ^ j
            chosen = came[0][g]
            for k in range(1, size):
                chosen = jnp.where(pick == k, came[k][g], chosen)
            ordered.append(chosen.astype(F32))
        row = lambda j, n: ordered[j][8 * n : 8 * n + 8, :]
        added = [row(j, nstate) + row(j, nstate + 1) for j in range(size)]
        zero = jnp.zeros((8, LANES), F32)
        running, prefix = added[0], zero
        for j in range(1, size):
            prefix = jnp.where(mine == j, running, prefix)
            running = running + added[j]
        total_rows = []
        for n in range(nstate):
            rate = rate_s[n]
            state, before = row(0, n), zero
            for j in range(1, size):
                before = jnp.where(mine == j, state, before)
                if j < size - 1 or not last:
                    state = state * jnp.exp2(rate * added[j]) + row(j, n)
            if not first:
                before = before * jnp.exp2(rate * old_sum_ref[g]) + old_ref[g, 8 * n : 8 * n + 8, :]
            refs[0][g, 8 * n : 8 * n + 8, :] = before
            total_rows.append(state)
        if not last:
            refs[1][g] = prefix if first else prefix + old_sum_ref[g]
            high = running.astype(BF16).astype(F32)
            refs[2][g] = jnp.concatenate(total_rows + [high, running - high], axis=0).astype(BF16)


def joined(message, a_log, beside):
    nstate = a_log.shape[0]
    groups = message.shape[0]
    place = lax.axis_index("seq")
    count = lax.axis_size("seq")
    smem = pl.BlockSpec(memory_space=pltpu.SMEM)
    vmem = pl.BlockSpec(memory_space=pltpu.VMEM)
    stride = 1
    old = []
    results = []
    sizes = (4, 2, 4, 4)
    for stage, (size, work) in enumerate(zip(sizes, beside)):
        first, last = stage == 0, stage == len(sizes) - 1
        mine = ((place // stride) % size).astype(jnp.int32).reshape(1)
        came = [message]
        for k in range(1, size):
            pairs = [(i, i ^ (k * stride)) for i in range(count)]
            came.append(lax.ppermute(message, "seq", pairs))
        done = [piece(message) for piece in work]
        if done:
            came, done = lax.optimization_barrier((came, done))
        results.extend(done)
        shapes = [jax.ShapeDtypeStruct((groups, 8 * nstate, LANES), F32)]
        if not last:
            shapes += [jax.ShapeDtypeStruct((groups, 8, LANES), F32), jax.ShapeDtypeStruct(message.shape, BF16)]
        outs = pl.pallas_call(
            functools.partial(join_kernel, size, first, last),
            in_specs=[smem] + [vmem] * (1 + size + len(old)),
            out_specs=[vmem] * len(shapes),
            out_shape=shapes,
            scratch_shapes=[pltpu.VMEM((nstate, 8, LANES), F32)],
            compiler_params=params(24),
            cost_estimate=cost(1e8, message.size * 2 * size, message.size * size),
            name="join",
        )(mine, a_log, *came, *old)
        if not last:
            old = [outs[1], outs[0]]
            message = outs[2]
        stride *= size
    return outs[0], results


def payload_kernel(turn_ref, own_ref, z1_ref, z2_ref, *outs):
    for step, out_ref in enumerate(outs, 1):
        out_ref[0] = z1_ref[...]
        wraps = turn_ref[0] + step >= 4

        @pl.when(wraps)
        def _():
            out_ref[1] = z2_ref[...]

        @pl.when(jnp.logical_not(wraps))
        def _():
            out_ref[1] = own_ref[...]


def payloads(turn, own, z1, z2):
    smem = pl.BlockSpec(memory_space=pltpu.SMEM)
    vmem = pl.BlockSpec(memory_space=pltpu.VMEM)
    return pl.pallas_call(
        payload_kernel,
        in_specs=[smem, vmem, vmem, vmem],
        out_specs=[vmem] * 3,
        out_shape=[jax.ShapeDtypeStruct((2,) + own.shape, BF16)] * 3,
        compiler_params=params(32),
        cost_estimate=cost(0, own.size * 18, 0),
        name="payload",
    )(turn, own, z1, z2)


def prepare_kernel(first_ref, turn_ref, own_ref, z1_ref, z2_ref, r1_ref, r2_ref, r3_ref, key_ref, value_ref):
    rows = own_ref.shape[1]
    local_kv = own_ref.shape[0] // (2 * HEAD_DIM)
    tiles = WINDOW // rows + 1
    first = first_ref[0]
    turn = turn_ref[0]
    pad = LANES - HEAD_DIM
    line = lax.broadcasted_iota(jnp.int32, (pad, rows), 0)
    empty = jnp.zeros((rows, pad), BF16)
    moved = (None, r1_ref, r2_ref, r3_ref)
    for tile in range(tiles):
        at = slice(tile * rows, (tile + 1) * rows)
        if tile % 4 == 0:
            block = (z2_ref, z1_ref, own_ref)[tile // 4][...]
        else:
            step = 4 - tile % 4
            early = tile < 4
            block = moved[step][jnp.where((turn < step) == early, 1, 0)]
        extra = jnp.where(line == 0, jnp.where(tile < first, LOW, 0.0), 0.0).astype(BF16)
        for head in range(local_kv):
            key = block[head * HEAD_DIM : (head + 1) * HEAD_DIM, :]
            value = block[(local_kv + head) * HEAD_DIM : (local_kv + head + 1) * HEAD_DIM, :]
            key_ref[head, :, at] = jnp.concatenate((key, extra), axis=0)
            turned = jnp.transpose(value.astype(F32)).astype(BF16)
            value_ref[head, at, :] = jnp.concatenate((turned, empty), axis=1)


def prepare(first, turn, own, z1, z2, moved):
    rows = own.shape[1]
    local_kv = own.shape[0] // (2 * HEAD_DIM)
    span = WINDOW + rows
    smem = pl.BlockSpec(memory_space=pltpu.SMEM)
    vmem = pl.BlockSpec(memory_space=pltpu.VMEM)
    return pl.pallas_call(
        prepare_kernel,
        in_specs=[smem, smem] + [vmem] * 6,
        out_specs=[vmem, vmem],
        out_shape=[
            jax.ShapeDtypeStruct((local_kv, LANES, span), BF16),
            jax.ShapeDtypeStruct((local_kv, span, LANES), BF16),
        ],
        compiler_params=params(32),
        cost_estimate=cost(1e9, own.size * 18, 0),
        name="prepare",
    )(first, turn, own, z1, z2, *moved)


def attention_kernel(q_ref, key_ref, value_ref, after_ref, out_ref, score_a, score_b):
    rows, width = q_ref.shape
    span = key_ref.shape[2]
    tiles = span // rows
    heads = width // HEAD_DIM
    lane = lax.broadcasted_iota(jnp.int32, (rows, LANES - HEAD_DIM), 1)
    one = jnp.where(lane == 0, 1.0, 0.0).astype(BF16)
    qpos = lax.broadcasted_iota(jnp.int32, (rows, rows), 0)
    cpos = lax.broadcasted_iota(jnp.int32, (rows, rows), 1)
    factor = HEAD_DIM ** (-0.5) * LOG2E
    store = (score_a, score_b)

    def query_of(head):
        return jnp.concatenate((q_ref[:, head * HEAD_DIM : (head + 1) * HEAD_DIM], one), axis=1)

    def scored(query, head, tile, top):
        at = slice(tile * rows, (tile + 1) * rows)
        score = jnp.dot(query, key_ref[0, :, at], preferred_element_type=F32)
        if tile == 0:
            score = jnp.where(cpos > qpos, score, -jnp.inf)
        if tile == tiles - 1:
            score = jnp.where(cpos <= qpos, score, -jnp.inf)
        store[head % 2][:, at] = score
        for piece in range(rows // LANES):
            top = jnp.maximum(top, score[:, piece * LANES : (piece + 1) * LANES])
        return top

    low = jnp.full((rows, LANES), -jnp.inf, F32)
    top = low
    query = query_of(0)
    for tile in range(tiles):
        top = scored(query, 0, tile, top)
    for head in range(heads):
        best = jnp.max(top, axis=1, keepdims=True)
        total = jnp.zeros((rows, LANES), F32)
        mixed = jnp.zeros((rows, LANES), F32)
        top = low
        if head + 1 < heads:
            query = query_of(head + 1)
        for tile in range(tiles):
            at = slice(tile * rows, (tile + 1) * rows)
            if head + 1 < heads:
                top = scored(query, head + 1, tile, top)
            prob = jnp.exp2((store[head % 2][:, at] - best) * factor)
            for piece in range(rows // LANES):
                total = total + prob[:, piece * LANES : (piece + 1) * LANES]
            mixed = mixed + jnp.dot(prob.astype(BF16), value_ref[0, at, :], preferred_element_type=F32)
        result = mixed / jnp.sum(total, axis=1, keepdims=True)
        out_ref[:, head * HEAD_DIM : (head + 1) * HEAD_DIM] = result[:, :HEAD_DIM].astype(BF16)


def attention_piece(queries, key, value, piece, after):
    rows = queries.shape[0]
    local_kv, _, span = key.shape
    heads = queries.shape[1] // HEAD_DIM
    share = heads // PIECES
    kv = piece * share // (heads // local_kv)
    pairs = rows * span * share
    return pl.pallas_call(
        attention_kernel,
        grid=(1,),
        in_specs=[
            pl.BlockSpec((rows, share * HEAD_DIM), lambda i: (0, piece)),
            pl.BlockSpec((1, LANES, span), lambda i: (kv, 0, 0)),
            pl.BlockSpec((1, span, LANES), lambda i: (kv, 0, 0)),
            pl.BlockSpec(memory_space=pl.ANY),
        ],
        out_specs=pl.BlockSpec((rows, share * HEAD_DIM), lambda i: (0, 0)),
        out_shape=jax.ShapeDtypeStruct((rows, share * HEAD_DIM), BF16),
        scratch_shapes=[pltpu.VMEM((rows, span), F32), pltpu.VMEM((rows, span), F32)],
        compiler_params=params(24),
        cost_estimate=cost(pairs * 2600, rows * 4096, pairs),
        name="attention",
    )(queries, key, value, after)


def local(
    mamba_in, mamba_gate, conv_weight, conv_bias, x_proj, dt_proj, dt_bias, a_log, d_skip,
    queries, keys, att_values, logits, targets, allowed,
):
    rows, channels = mamba_in.shape
    taps = conv_weight.shape[0]
    nstate = a_log.shape[0]
    subs = channels // LANES
    place = lax.axis_index("seq")
    count = lax.axis_size("seq")
    rim = shifted(mamba_in[rows - (taps - 1) :], "seq", 1)
    own = jnp.concatenate((keys.T, att_values.T), axis=0)
    z1 = shifted(own, "seq", 4)
    z2 = shifted(own, "seq", 8)
    first = jnp.maximum(WINDOW // rows - place, 0).astype(jnp.int32).reshape(1)
    turn = (place % 4).astype(jnp.int32).reshape(1)
    sent = payloads(turn, own, z1, z2)
    moved = []
    for step, payload in enumerate(sent, 1):
        pairs = [(i, i - i % 4 + (i + step) % 4) for i in range(count)]
        moved.append(lax.ppermute(payload, "seq", pairs))
    conv_out, part = convolve(mamba_in, rim, conv_weight, conv_bias, x_proj.T)
    other = swapped(part)
    y, cum, message = local_scan(part, other, dt_proj, dt_bias, a_log, d_skip, conv_out, sent[2])
    made = {}

    def score(message):
        return scoring_part(logits, targets, allowed, [message] + moved)

    def attend(piece):
        def run(message):
            if not made:
                made["kv"] = prepare(first, turn, own, z1, z2, moved)
            return attention_piece(queries, *made["kv"], piece, message)

        return run

    incoming, results = joined(message, a_log, [[score], [attend(0)], [attend(1), attend(2)], [attend(3)]])
    stats = results[0]
    attention_out = jnp.concatenate(results[1:], axis=1)
    loglik = scoring_join(stats, swapped(stats))
    mamba_out = finish(y, cum, part, other, incoming, a_log, mamba_gate)
    return (mamba_out, attention_out, loglik)


def solution(mesh):
    in_specs = (
        P("seq", "vocab"),
        P("seq", "vocab"),
        P(None, "vocab"),
        P("vocab"),
        P("vocab", None),
        P(None, "vocab"),
        P("vocab"),
        P(None, "vocab"),
        P("vocab"),
        P("seq", "vocab"),
        P("seq", "vocab"),
        P("seq", "vocab"),
        P("seq", "vocab"),
        P("seq"),
        P("seq", "vocab"),
    )
    out_specs = (P("seq", "vocab"), P("seq", "vocab"), P("seq"))
    return jax.shard_map(local, mesh=mesh, in_specs=in_specs, out_specs=out_specs, check_vma=False)
```

```python
import functools

import jax
import jax.numpy as jnp
from jax import lax
from jax.experimental import pallas as pl
from jax.experimental.pallas import tpu as pltpu
from jax.sharding import PartitionSpec as P

HEADS = 32
KV_HEADS = 4
HEAD_DIM = 96
WINDOW = 2048
LOG2E = 1.4426950408889634
F32 = jnp.float32
BF16 = jnp.bfloat16
GROUP = 1024
LANES = 128
LOW = -1e30
PIECES = 4
TOKENS = 16


def params(mib):
    return pltpu.CompilerParams(vmem_limit_bytes=mib * 1024 * 1024)


def cost(flops, nbytes, trans=0):
    return pl.CostEstimate(flops=int(flops), bytes_accessed=int(nbytes), transcendentals=int(trans))


def shifted(value, axis, steps):
    count = lax.axis_size(axis)
    leading, last = (max(0, -steps), min(count, count - steps))
    return lax.ppermute(value, axis, [(source, source + steps) for source in range(leading, last)])


def swapped(value):
    return lax.ppermute(value, "vocab", [(0, 1), (1, 0)])


def score_kernel(logits_ref, allowed_ref, local_target_ref, *refs):
    out_ref = refs[-1]
    rows, width = logits_ref.shape
    words = LANES
    span = words * 8
    row_id = lax.broadcasted_iota(jnp.int32, (words, span), 0)
    col_id = lax.broadcasted_iota(jnp.int32, (words, span), 1)
    expand = jnp.where(row_id == col_id // 8, 1.0, 0.0).astype(BF16)
    col = lax.broadcasted_iota(jnp.int32, (rows, span), 1)
    bit = jnp.left_shift(jnp.int32(1), col & 7)
    wanted = local_target_ref[...]
    top = jnp.full((rows, LANES), -jnp.inf, F32)
    target = jnp.zeros((rows, LANES), F32)
    parts = []
    for block in range(width // span):
        values = logits_ref[:, block * span : (block + 1) * span].astype(F32)
        word = allowed_ref[:, block * words : (block + 1) * words].astype(F32).astype(BF16)
        spread = jnp.dot(word, expand, preferred_element_type=F32).astype(jnp.int32)
        masked = jnp.where((spread & bit) != 0, values, -jnp.inf)
        hit = jnp.where(col == wanted - block * span, values, 0.0)
        for piece in range(8):
            at = slice(piece * LANES, (piece + 1) * LANES)
            top = jnp.maximum(top, masked[:, at])
            target = target + hit[:, at]
        parts.append(masked)
    best = jnp.maximum(jnp.max(top, axis=1, keepdims=True), LOW)
    total = jnp.zeros((rows, LANES), F32)
    for masked in parts:
        terms = jnp.exp(masked - best)
        for piece in range(8):
            total = total + terms[:, piece * LANES : (piece + 1) * LANES]
    summed = jnp.sum(total, axis=1, keepdims=True)
    found = jnp.sum(target, axis=1, keepdims=True)
    lane = lax.broadcasted_iota(jnp.int32, (rows, LANES), 1)
    out_ref[...] = jnp.where(lane == 0, best, jnp.where(lane == 1, summed, found))


def scoring_part(logits, targets, allowed, after):
    rows, width = logits.shape
    block = 64
    local_target = (targets - lax.axis_index("vocab") * width).reshape(rows, 1)
    stats = pl.pallas_call(
        score_kernel,
        grid=(rows // block,),
        in_specs=[
            pl.BlockSpec((block, width), lambda i: (i, 0)),
            pl.BlockSpec((block, width // 8), lambda i: (i, 0)),
            pl.BlockSpec((block, 1), lambda i: (i, 0)),
        ]
        + [pl.BlockSpec(memory_space=pl.ANY)] * len(after),
        out_specs=pl.BlockSpec((block, LANES), lambda i: (i, 0)),
        out_shape=jax.ShapeDtypeStruct((rows, LANES), F32),
        compiler_params=params(16),
        cost_estimate=cost(rows * width * 256, rows * width * 3, rows * width),
        name="scoring",
    )(logits, allowed, local_target, *after)
    return stats[:, :8].T


def scoring_join(mine, other):
    top = jnp.maximum(mine[0], other[0])
    total = mine[1] * jnp.exp(mine[0] - top) + other[1] * jnp.exp(other[0] - top)
    return mine[2] + other[2] - top - jnp.log(total)


def conv_kernel(x_ref, rim_ref, weight_ref, bias_ref, proj_ref, conv_ref, out_ref, pad):
    rows = x_ref.shape[0]
    taps = weight_ref.shape[0]
    x = x_ref[...].astype(F32)
    pad[8 : 8 + rows, :] = x
    pad[8 - (taps - 1) : 8, :] = rim_ref[...].astype(F32)
    conv = bias_ref[...]
    for tap in range(taps):
        start = 8 - (taps - 1) + tap
        conv = conv + weight_ref[tap : tap + 1, :] * pad[start : start + rows, :]
    value = (conv / (1.0 + jnp.exp(-conv))).astype(BF16)
    conv_ref[...] = value
    part = lax.dot_general(value, proj_ref[...], (((1,), (1,)), ((), ())), preferred_element_type=F32)

    @pl.when(pl.program_id(0) == 0)
    def _():
        out_ref[...] = part

    @pl.when(pl.program_id(0) > 0)
    def _():
        out_ref[...] += part


def convolve(mamba_in, rim, conv_weight, conv_bias, x_proj):
    rows, channels = mamba_in.shape
    taps = conv_weight.shape[0]
    width = x_proj.shape[0]
    block = 1024
    return pl.pallas_call(
        conv_kernel,
        grid=(channels // block,),
        in_specs=[
            pl.BlockSpec((rows, block), lambda i: (0, i)),
            pl.BlockSpec((taps - 1, block), lambda i: (0, i)),
            pl.BlockSpec((taps, block), lambda i: (0, i)),
            pl.BlockSpec((1, block), lambda i: (0, i)),
            pl.BlockSpec((width, block), lambda i: (0, i)),
        ],
        out_specs=[
            pl.BlockSpec((rows, block), lambda i: (0, i)),
            pl.BlockSpec((rows, width), lambda i: (0, 0)),
        ],
        out_shape=[
            jax.ShapeDtypeStruct((rows, channels), BF16),
            jax.ShapeDtypeStruct((rows, width), F32),
        ],
        scratch_shapes=[pltpu.VMEM((rows + 8, block), F32)],
        compiler_params=params(60),
        cost_estimate=cost(rows * channels * 700, rows * channels * 4, rows * channels * 2),
        name="convolution",
    )(mamba_in, rim, conv_weight, conv_bias.reshape(1, channels), x_proj)


def softplus(v):
    e = jnp.exp(-jnp.abs(v))
    return jnp.maximum(v, 0.0) + jnp.log1p(e)


def spread(table, wide_s, rows):
    for n in range(table.shape[1]):
        wide_s[n * rows : (n + 1) * rows, :] = jnp.broadcast_to(table[:, n : n + 1], (rows, LANES))


def fold_rates(alog_ref, rate_s, group):
    for sub in range(8):
        at = slice(group * GROUP + sub * LANES, group * GROUP + (sub + 1) * LANES)
        rate_s[:, sub, :] = -LOG2E * jnp.exp(alog_ref[:, at])


def scan_kernel(
    mine_ref, other_ref, dt_ref, bias_ref, alog_ref, skip_ref, conv_ref, after_ref,
    y_ref, cum_ref, message_ref, delta_s, x_s, wide_s, rate_s,
):
    rows, rank = mine_ref.shape[0], dt_ref.shape[0]
    nstate = alog_ref.shape[0]
    spread(mine_ref[:, rank:] + other_ref[:, rank:], wide_s, rows)
    low = (mine_ref[:, :rank] + other_ref[:, :rank]).astype(BF16)
    for group in range(conv_ref.shape[1] // GROUP):
        here = slice(8 * group, 8 * group + 8)
        for sub in range(8):
            at = slice(group * GROUP + sub * LANES, group * GROUP + (sub + 1) * LANES)
            product = jnp.dot(low, dt_ref[:, at], preferred_element_type=F32)
            delta_s[:, sub, :] = softplus(product + bias_ref[:, at])
            x_s[:, sub, :] = conv_ref[:, at].astype(F32)
        fold_rates(alog_ref, rate_s, group)

        def step(block, carry):
            cum, state = carry
            start = block * TOKENS
            ds = [delta_s[start + k] for k in range(TOKENS)]
            xs = [x_s[start + k] for k in range(TOKENS)]
            cums, ys = [], []
            for k in range(TOKENS):
                cum = cum + ds[k]
                dx = ds[k] * xs[k]
                sums = [skip_ref[here, :] * xs[k], jnp.zeros_like(cum)]
                new = []
                for n in range(nstate):
                    row = n * rows + start + k
                    h = jnp.exp2(ds[k] * rate_s[n]) * state[n] + dx * wide_s[pl.ds(row, 1), :]
                    sums[n % 2] = sums[n % 2] + h * wide_s[pl.ds(row + nstate * rows, 1), :]
                    new.append(h)
                state = tuple(new)
                cums.append(cum)
                ys.append(sums[0] + sums[1])
            for k in range(TOKENS):
                cum_ref[start + k, here, :] = cums[k]
                y_ref[start + k, here, :] = ys[k]
            return cum, state

        zero = jnp.zeros((8, LANES), F32)
        cum, state = lax.fori_loop(0, rows // TOKENS, step, (zero, (zero,) * nstate))
        high = cum.astype(BF16).astype(F32)
        message_ref[group] = jnp.concatenate(state + (high, cum - high), axis=0).astype(BF16)


def local_scan(mine, other, dt_proj, dt_bias, a_log, d_skip, conv_out, after):
    rows, channels = conv_out.shape
    nstate = a_log.shape[0]
    subs = channels // LANES
    vmem = pl.BlockSpec(memory_space=pltpu.VMEM)
    return pl.pallas_call(
        scan_kernel,
        in_specs=[vmem] * 7 + [pl.BlockSpec(memory_space=pl.ANY)],
        out_specs=[vmem] * 3,
        out_shape=[
            jax.ShapeDtypeStruct((rows, subs, LANES), F32),
            jax.ShapeDtypeStruct((rows, subs, LANES), F32),
            jax.ShapeDtypeStruct((channels // GROUP, 8 * (nstate + 2), LANES), BF16),
        ],
        scratch_shapes=[
            pltpu.VMEM((rows, 8, LANES), F32),
            pltpu.VMEM((rows, 8, LANES), F32),
            pltpu.VMEM((rows * nstate * 2, LANES), F32),
            pltpu.VMEM((nstate, 8, LANES), F32),
        ],
        compiler_params=params(24),
        cost_estimate=cost(rows * channels * nstate * 1600, rows * channels * 12, rows * channels * nstate),
        name="local_scan",
    )(
        mine, other, dt_proj, dt_bias.reshape(1, channels), a_log, d_skip.reshape(subs, LANES),
        conv_out, after,
    )


def finish_kernel(y_ref, cum_ref, mine_ref, other_ref, state_ref, alog_ref, gate_ref, out_ref, y_s, wide_s, rate_s):
    rows = y_ref.shape[0]
    nstate = alog_ref.shape[0]
    spot = mine_ref.shape[1] - nstate
    spread(mine_ref[:, spot:] + other_ref[:, spot:], wide_s, rows)
    for group in range(gate_ref.shape[1] // GROUP):
        here = slice(8 * group, 8 * group + 8)
        fold_rates(alog_ref, rate_s, group)

        def step(block, carry):
            start = block * TOKENS
            cums = [cum_ref[start + k, here, :] for k in range(TOKENS)]
            ys = [[y_ref[start + k, here, :], jnp.zeros((8, LANES), F32)] for k in range(TOKENS)]
            for n in range(nstate):
                rate, state = rate_s[n], state_ref[group, 8 * n : 8 * n + 8, :]
                for k in range(TOKENS):
                    term = (jnp.exp2(cums[k] * rate) * state) * wide_s[pl.ds(n * rows + start + k, 1), :]
                    ys[k][n % 2] = ys[k][n % 2] + term
            for k in range(TOKENS):
                y_s[start + k] = ys[k][0] + ys[k][1]
            return carry

        lax.fori_loop(0, rows // TOKENS, step, 0)
        for sub in range(8):
            at = slice(group * GROUP + sub * LANES, group * GROUP + (sub + 1) * LANES)
            half = 0.5 * gate_ref[:, at].astype(F32)
            out_ref[:, at] = (y_s[:, sub, :] * (half * jnp.tanh(half) + half)).astype(BF16)


def finish(y, cum, mine, other, incoming, a_log, mamba_gate):
    rows, channels = mamba_gate.shape
    nstate = a_log.shape[0]
    vmem = pl.BlockSpec(memory_space=pltpu.VMEM)
    return pl.pallas_call(
        finish_kernel,
        in_specs=[vmem] * 7,
        out_specs=vmem,
        out_shape=jax.ShapeDtypeStruct((rows, channels), BF16),
        scratch_shapes=[
            pltpu.VMEM((rows, 8, LANES), F32),
            pltpu.VMEM((rows * nstate, LANES), F32),
            pltpu.VMEM((nstate, 8, LANES), F32),
        ],
        compiler_params=params(24),
        cost_estimate=cost(rows * channels * nstate * 1000, rows * channels * 12, rows * channels * nstate),
        name="finish",
    )(y, cum, mine, other, incoming, a_log, mamba_gate)


def join_kernel(size, first, last, place_ref, alog_ref, *refs):
    came, rate_s, refs = refs[:size], refs[-1], refs[size:-1]
    if not first:
        old_sum_ref, old_ref, refs = refs[0], refs[1], refs[2:]
    nstate = alog_ref.shape[0]
    mine = place_ref[0]
    groups = came[0].shape[0]
    for g in range(groups):
        fold_rates(alog_ref, rate_s, g)
        ordered = []
        for j in range(size):
            pick = mine ^ j
            chosen = came[0][g]
            for k in range(1, size):
                chosen = jnp.where(pick == k, came[k][g], chosen)
            ordered.append(chosen.astype(F32))
        row = lambda j, n: ordered[j][8 * n : 8 * n + 8, :]
        added = [row(j, nstate) + row(j, nstate + 1) for j in range(size)]
        zero = jnp.zeros((8, LANES), F32)
        running, prefix = added[0], zero
        for j in range(1, size):
            prefix = jnp.where(mine == j, running, prefix)
            running = running + added[j]
        total_rows = []
        for n in range(nstate):
            rate = rate_s[n]
            state, before = row(0, n), zero
            for j in range(1, size):
                before = jnp.where(mine == j, state, before)
                if j < size - 1 or not last:
                    state = state * jnp.exp2(rate * added[j]) + row(j, n)
            if not first:
                before = before * jnp.exp2(rate * old_sum_ref[g]) + old_ref[g, 8 * n : 8 * n + 8, :]
            refs[0][g, 8 * n : 8 * n + 8, :] = before
            total_rows.append(state)
        if not last:
            refs[1][g] = prefix if first else prefix + old_sum_ref[g]
            high = running.astype(BF16).astype(F32)
            refs[2][g] = jnp.concatenate(total_rows + [high, running - high], axis=0).astype(BF16)


def joined(message, a_log, beside):
    nstate = a_log.shape[0]
    groups = message.shape[0]
    place = lax.axis_index("seq")
    count = lax.axis_size("seq")
    smem = pl.BlockSpec(memory_space=pltpu.SMEM)
    vmem = pl.BlockSpec(memory_space=pltpu.VMEM)
    stride = 1
    old = []
    results = []
    sizes = (4, 2, 4, 4)
    for stage, (size, work) in enumerate(zip(sizes, beside)):
        first, last = stage == 0, stage == len(sizes) - 1
        mine = ((place // stride) % size).astype(jnp.int32).reshape(1)
        came = [message]
        for k in range(1, size):
            pairs = [(i, i ^ (k * stride)) for i in range(count)]
            came.append(lax.ppermute(message, "seq", pairs))
        done = []
        for spot, piece in enumerate(work):
            done.append(piece(done[-1] if spot else came[1] if len(work) > 1 else message))
        if done:
            came, done = lax.optimization_barrier((came, done))
        results.extend(done)
        shapes = [jax.ShapeDtypeStruct((groups, 8 * nstate, LANES), F32)]
        if not last:
            shapes += [jax.ShapeDtypeStruct((groups, 8, LANES), F32), jax.ShapeDtypeStruct(message.shape, BF16)]
        outs = pl.pallas_call(
            functools.partial(join_kernel, size, first, last),
            in_specs=[smem] + [vmem] * (1 + size + len(old)),
            out_specs=[vmem] * len(shapes),
            out_shape=shapes,
            scratch_shapes=[pltpu.VMEM((nstate, 8, LANES), F32)],
            compiler_params=params(16),
            cost_estimate=cost(1e8, message.size * 2 * size, message.size * size),
            name="join",
        )(mine, a_log, *came, *old)
        if not last:
            old = [outs[1], outs[0]]
            message = outs[2]
        stride *= size
    return outs[0], results


def payload_kernel(turn_ref, own_ref, z1_ref, z2_ref, *outs):
    for step, out_ref in enumerate(outs, 1):
        out_ref[0] = z1_ref[...]
        wraps = turn_ref[0] + step >= 4

        @pl.when(wraps)
        def _():
            out_ref[1] = z2_ref[...]

        @pl.when(jnp.logical_not(wraps))
        def _():
            out_ref[1] = own_ref[...]


def payloads(turn, own, z1, z2):
    smem = pl.BlockSpec(memory_space=pltpu.SMEM)
    vmem = pl.BlockSpec(memory_space=pltpu.VMEM)
    return pl.pallas_call(
        payload_kernel,
        in_specs=[smem, vmem, vmem, vmem],
        out_specs=[vmem] * 3,
        out_shape=[jax.ShapeDtypeStruct((2,) + own.shape, BF16)] * 3,
        compiler_params=params(16),
        cost_estimate=cost(0, own.size * 18, 0),
        name="payload",
    )(turn, own, z1, z2)


def prepare_kernel(first_ref, turn_ref, own_ref, z1_ref, z2_ref, r1_ref, r2_ref, r3_ref, key_ref, value_ref):
    rows = own_ref.shape[1]
    local_kv = own_ref.shape[0] // (2 * HEAD_DIM)
    tiles = WINDOW // rows + 1
    first = first_ref[0]
    turn = turn_ref[0]
    pad = LANES - HEAD_DIM
    line = lax.broadcasted_iota(jnp.int32, (pad, rows), 0)
    empty = jnp.zeros((rows, pad), BF16)
    moved = (None, r1_ref, r2_ref, r3_ref)
    for tile in range(tiles):
        at = slice(tile * rows, (tile + 1) * rows)
        if tile % 4 == 0:
            block = (z2_ref, z1_ref, own_ref)[tile // 4][...]
        else:
            step = 4 - tile % 4
            early = tile < 4
            block = moved[step][jnp.where((turn < step) == early, 1, 0)]
        extra = jnp.where(line == 0, jnp.where(tile < first, LOW, 0.0), 0.0).astype(BF16)
        for head in range(local_kv):
            key = block[head * HEAD_DIM : (head + 1) * HEAD_DIM, :]
            value = block[(local_kv + head) * HEAD_DIM : (local_kv + head + 1) * HEAD_DIM, :]
            key_ref[head, :, at] = jnp.concatenate((key, extra), axis=0)
            turned = jnp.transpose(value.astype(F32)).astype(BF16)
            value_ref[head, at, :] = jnp.concatenate((turned, empty), axis=1)


def prepare(first, turn, own, z1, z2, moved):
    rows = own.shape[1]
    local_kv = own.shape[0] // (2 * HEAD_DIM)
    span = WINDOW + rows
    smem = pl.BlockSpec(memory_space=pltpu.SMEM)
    vmem = pl.BlockSpec(memory_space=pltpu.VMEM)
    return pl.pallas_call(
        prepare_kernel,
        in_specs=[smem, smem] + [vmem] * 6,
        out_specs=[vmem, vmem],
        out_shape=[
            jax.ShapeDtypeStruct((local_kv, LANES, span), BF16),
            jax.ShapeDtypeStruct((local_kv, span, LANES), BF16),
        ],
        compiler_params=params(16),
        cost_estimate=cost(1e9, own.size * 18, 0),
        name="prepare",
    )(first, turn, own, z1, z2, *moved)


def attention_kernel(q_ref, key_ref, value_ref, after_ref, *refs):
    earlier, (out_ref, score_a, score_b) = refs[:-3], refs[-3:]
    rows, width = q_ref.shape
    span = key_ref.shape[2]
    tiles = span // rows
    heads = width // HEAD_DIM
    lane = lax.broadcasted_iota(jnp.int32, (rows, LANES - HEAD_DIM), 1)
    one = jnp.where(lane == 0, 1.0, 0.0).astype(BF16)
    qpos = lax.broadcasted_iota(jnp.int32, (rows, rows), 0)
    cpos = lax.broadcasted_iota(jnp.int32, (rows, rows), 1)
    factor = HEAD_DIM ** (-0.5) * LOG2E
    store = (score_a, score_b)

    base = sum(ref.shape[1] for ref in earlier)
    spot = 0
    for ref in earlier:
        out_ref[:, spot : spot + ref.shape[1]] = ref[...]
        spot += ref.shape[1]

    def query_of(head):
        return jnp.concatenate((q_ref[:, head * HEAD_DIM : (head + 1) * HEAD_DIM], one), axis=1)

    def scored(query, head, tile, top):
        at = slice(tile * rows, (tile + 1) * rows)
        score = jnp.dot(query, key_ref[0, :, at], preferred_element_type=F32)
        if tile == 0:
            score = jnp.where(cpos > qpos, score, -jnp.inf)
        if tile == tiles - 1:
            score = jnp.where(cpos <= qpos, score, -jnp.inf)
        store[head % 2][:, at] = score
        for piece in range(rows // LANES):
            top = jnp.maximum(top, score[:, piece * LANES : (piece + 1) * LANES])
        return top

    low = jnp.full((rows, LANES), -jnp.inf, F32)
    top = low
    query = query_of(0)
    for tile in range(tiles):
        top = scored(query, 0, tile, top)
    for head in range(heads):
        best = jnp.max(top, axis=1, keepdims=True)
        total = jnp.zeros((rows, LANES), F32)
        mixed = jnp.zeros((rows, LANES), F32)
        top = low
        if head + 1 < heads:
            query = query_of(head + 1)
        for tile in range(tiles):
            at = slice(tile * rows, (tile + 1) * rows)
            if head + 1 < heads:
                top = scored(query, head + 1, tile, top)
            prob = jnp.exp2((store[head % 2][:, at] - best) * factor)
            for piece in range(rows // LANES):
                total = total + prob[:, piece * LANES : (piece + 1) * LANES]
            mixed = mixed + jnp.dot(prob.astype(BF16), value_ref[0, at, :], preferred_element_type=F32)
        result = mixed / jnp.sum(total, axis=1, keepdims=True)
        at = slice(base + head * HEAD_DIM, base + (head + 1) * HEAD_DIM)
        out_ref[:, at] = result[:, :HEAD_DIM].astype(BF16)


def attention_piece(queries, key, value, piece, after, earlier):
    rows = queries.shape[0]
    local_kv, _, span = key.shape
    heads = queries.shape[1] // HEAD_DIM
    share = heads // PIECES
    kv = piece * share // (heads // local_kv)
    pairs = rows * span * share
    width = share * HEAD_DIM * (1 + len(earlier))
    return pl.pallas_call(
        attention_kernel,
        grid=(1,),
        in_specs=[
            pl.BlockSpec((rows, share * HEAD_DIM), lambda i: (0, piece)),
            pl.BlockSpec((1, LANES, span), lambda i: (kv, 0, 0)),
            pl.BlockSpec((1, span, LANES), lambda i: (kv, 0, 0)),
            pl.BlockSpec(memory_space=pl.ANY),
        ]
        + [pl.BlockSpec((rows, share * HEAD_DIM), lambda i: (0, 0))] * len(earlier),
        out_specs=pl.BlockSpec((rows, width), lambda i: (0, 0)),
        out_shape=jax.ShapeDtypeStruct((rows, width), BF16),
        scratch_shapes=[pltpu.VMEM((rows, span), F32), pltpu.VMEM((rows, span), F32)],
        compiler_params=params(16),
        cost_estimate=cost(pairs * 2600, rows * 4096, pairs),
        name="attention",
    )(queries, key, value, after, *earlier)


def local(
    mamba_in, mamba_gate, conv_weight, conv_bias, x_proj, dt_proj, dt_bias, a_log, d_skip,
    queries, keys, att_values, logits, targets, allowed,
):
    rows, channels = mamba_in.shape
    taps = conv_weight.shape[0]
    nstate = a_log.shape[0]
    subs = channels // LANES
    place = lax.axis_index("seq")
    count = lax.axis_size("seq")
    rim = shifted(mamba_in[rows - (taps - 1) :], "seq", 1)
    own = jnp.concatenate((keys.T, att_values.T), axis=0)
    z1 = shifted(own, "seq", 4)
    z2 = shifted(own, "seq", 8)
    first = jnp.maximum(WINDOW // rows - place, 0).astype(jnp.int32).reshape(1)
    turn = (place % 4).astype(jnp.int32).reshape(1)
    sent = payloads(turn, own, z1, z2)
    moved = []
    for step, payload in enumerate(sent, 1):
        pairs = [(i, i - i % 4 + (i + step) % 4) for i in range(count)]
        moved.append(lax.ppermute(payload, "seq", pairs))
    conv_out, part = convolve(mamba_in, rim, conv_weight, conv_bias, x_proj.T)
    other = swapped(part)
    y, cum, message = local_scan(part, other, dt_proj, dt_bias, a_log, d_skip, conv_out, sent[2])
    made = {}

    def score(message):
        return scoring_part(logits, targets, allowed, [message] + moved)

    def attend(piece):
        def run(message):
            if not made:
                made["kv"] = prepare(first, turn, own, z1, z2, moved)
            pieces = made.setdefault("out", [])
            earlier = pieces if piece == PIECES - 1 else []
            pieces.append(attention_piece(queries, *made["kv"], piece, message, earlier))
            return pieces[-1]

        return run

    incoming, results = joined(message, a_log, [[score], [attend(0)], [attend(1), attend(2)], [attend(3)]])
    stats = results[0]
    attention_out = results[-1]
    others = swapped(stats)
    stats, others, attention_out = lax.optimization_barrier((stats, others, attention_out))
    loglik = scoring_join(stats, others)
    mamba_out = finish(y, cum, part, other, incoming, a_log, mamba_gate)
    return (mamba_out, attention_out, loglik)


def solution(mesh):
    in_specs = (
        P("seq", "vocab"),
        P("seq", "vocab"),
        P(None, "vocab"),
        P("vocab"),
        P("vocab", None),
        P(None, "vocab"),
        P("vocab"),
        P(None, "vocab"),
        P("vocab"),
        P("seq", "vocab"),
        P("seq", "vocab"),
        P("seq", "vocab"),
        P("seq", "vocab"),
        P("seq"),
        P("seq", "vocab"),
    )
    out_specs = (P("seq", "vocab"), P("seq", "vocab"), P("seq"))
    return jax.shard_map(local, mesh=mesh, in_specs=in_specs, out_specs=out_specs, check_vma=False)
```

```python
import functools

import jax
import jax.numpy as jnp
from jax import lax
from jax.experimental import pallas as pl
from jax.experimental.pallas import tpu as pltpu
from jax.sharding import PartitionSpec as P

HEADS = 32
KV_HEADS = 4
HEAD_DIM = 96
WINDOW = 2048
LOG2E = 1.4426950408889634
F32 = jnp.float32
BF16 = jnp.bfloat16
GROUP = 1024
LANES = 128
LOW = -1e30
PIECES = 4
TOKENS = 16


def params(mib):
    return pltpu.CompilerParams(vmem_limit_bytes=mib * 1024 * 1024)


def cost(flops, nbytes, trans=0):
    return pl.CostEstimate(flops=int(flops), bytes_accessed=int(nbytes), transcendentals=int(trans))


def shifted(value, axis, steps):
    count = lax.axis_size(axis)
    leading, last = (max(0, -steps), min(count, count - steps))
    return lax.ppermute(value, axis, [(source, source + steps) for source in range(leading, last)])


def swapped(value):
    return lax.ppermute(value, "vocab", [(0, 1), (1, 0)])


def score_kernel(logits_ref, allowed_ref, local_target_ref, *refs):
    out_ref = refs[-1]
    rows, width = logits_ref.shape
    words = LANES
    span = words * 8
    row_id = lax.broadcasted_iota(jnp.int32, (words, span), 0)
    col_id = lax.broadcasted_iota(jnp.int32, (words, span), 1)
    expand = jnp.where(row_id == col_id // 8, 1.0, 0.0).astype(BF16)
    col = lax.broadcasted_iota(jnp.int32, (rows, span), 1)
    bit = jnp.left_shift(jnp.int32(1), col & 7)
    wanted = local_target_ref[...]
    top = jnp.full((rows, LANES), -jnp.inf, F32)
    target = jnp.zeros((rows, LANES), F32)
    parts = []
    for block in range(width // span):
        values = logits_ref[:, block * span : (block + 1) * span].astype(F32)
        word = allowed_ref[:, block * words : (block + 1) * words].astype(F32).astype(BF16)
        spread = jnp.dot(word, expand, preferred_element_type=F32).astype(jnp.int32)
        masked = jnp.where((spread & bit) != 0, values, -jnp.inf)
        hit = jnp.where(col == wanted - block * span, values, 0.0)
        for piece in range(8):
            at = slice(piece * LANES, (piece + 1) * LANES)
            top = jnp.maximum(top, masked[:, at])
            target = target + hit[:, at]
        parts.append(masked)
    best = jnp.maximum(jnp.max(top, axis=1, keepdims=True), LOW)
    total = jnp.zeros((rows, LANES), F32)
    for masked in parts:
        terms = jnp.exp(masked - best)
        for piece in range(8):
            total = total + terms[:, piece * LANES : (piece + 1) * LANES]
    summed = jnp.sum(total, axis=1, keepdims=True)
    found = jnp.sum(target, axis=1, keepdims=True)
    lane = lax.broadcasted_iota(jnp.int32, (rows, LANES), 1)
    out_ref[...] = jnp.where(lane == 0, best, jnp.where(lane == 1, summed, found))


def scoring_part(logits, targets, allowed, after):
    rows, width = logits.shape
    block = 64
    local_target = (targets - lax.axis_index("vocab") * width).reshape(rows, 1)
    stats = pl.pallas_call(
        score_kernel,
        grid=(rows // block,),
        in_specs=[
            pl.BlockSpec((block, width), lambda i: (i, 0)),
            pl.BlockSpec((block, width // 8), lambda i: (i, 0)),
            pl.BlockSpec((block, 1), lambda i: (i, 0)),
        ]
        + [pl.BlockSpec(memory_space=pl.ANY)] * len(after),
        out_specs=pl.BlockSpec((block, LANES), lambda i: (i, 0)),
        out_shape=jax.ShapeDtypeStruct((rows, LANES), F32),
        compiler_params=params(16),
        cost_estimate=cost(rows * width * 256, rows * width * 3, rows * width),
        name="scoring",
    )(logits, allowed, local_target, *after)
    return stats[:, :8].T


def scoring_join(mine, other):
    top = jnp.maximum(mine[0], other[0])
    total = mine[1] * jnp.exp(mine[0] - top) + other[1] * jnp.exp(other[0] - top)
    return mine[2] + other[2] - top - jnp.log(total)


def conv_kernel(x_ref, rim_ref, weight_ref, bias_ref, proj_ref, conv_ref, out_ref, pad):
    rows = x_ref.shape[0]
    taps = weight_ref.shape[0]
    x = x_ref[...].astype(F32)
    pad[8 : 8 + rows, :] = x
    pad[8 - (taps - 1) : 8, :] = rim_ref[...].astype(F32)
    conv = bias_ref[...]
    for tap in range(taps):
        start = 8 - (taps - 1) + tap
        conv = conv + weight_ref[tap : tap + 1, :] * pad[start : start + rows, :]
    value = (conv / (1.0 + jnp.exp(-conv))).astype(BF16)
    conv_ref[...] = value
    part = lax.dot_general(value, proj_ref[...], (((1,), (1,)), ((), ())), preferred_element_type=F32)

    @pl.when(pl.program_id(0) == 0)
    def _():
        out_ref[...] = part

    @pl.when(pl.program_id(0) > 0)
    def _():
        out_ref[...] += part


def convolve(mamba_in, rim, conv_weight, conv_bias, x_proj):
    rows, channels = mamba_in.shape
    taps = conv_weight.shape[0]
    width = x_proj.shape[0]
    block = 1024
    return pl.pallas_call(
        conv_kernel,
        grid=(channels // block,),
        in_specs=[
            pl.BlockSpec((rows, block), lambda i: (0, i)),
            pl.BlockSpec((taps - 1, block), lambda i: (0, i)),
            pl.BlockSpec((taps, block), lambda i: (0, i)),
            pl.BlockSpec((1, block), lambda i: (0, i)),
            pl.BlockSpec((width, block), lambda i: (0, i)),
        ],
        out_specs=[
            pl.BlockSpec((rows, block), lambda i: (0, i)),
            pl.BlockSpec((rows, width), lambda i: (0, 0)),
        ],
        out_shape=[
            jax.ShapeDtypeStruct((rows, channels), BF16),
            jax.ShapeDtypeStruct((rows, width), F32),
        ],
        scratch_shapes=[pltpu.VMEM((rows + 8, block), F32)],
        compiler_params=params(60),
        cost_estimate=cost(rows * channels * 700, rows * channels * 4, rows * channels * 2),
        name="convolution",
    )(mamba_in, rim, conv_weight, conv_bias.reshape(1, channels), x_proj)


def softplus(v):
    e = jnp.exp(-jnp.abs(v))
    return jnp.maximum(v, 0.0) + jnp.log1p(e)


def spread(table, wide_s, rows):
    for n in range(table.shape[1]):
        wide_s[n * rows : (n + 1) * rows, :] = jnp.broadcast_to(table[:, n : n + 1], (rows, LANES))


def fold_rates(alog_ref, rate_s, group):
    for sub in range(8):
        at = slice(group * GROUP + sub * LANES, group * GROUP + (sub + 1) * LANES)
        rate_s[:, sub, :] = -LOG2E * jnp.exp(alog_ref[:, at])


def scan_kernel(
    mine_ref, other_ref, dt_ref, bias_ref, alog_ref, skip_ref, conv_ref, after_ref,
    y_ref, cum_ref, message_ref, delta_s, x_s, wide_s, rate_s,
):
    rows, rank = mine_ref.shape[0], dt_ref.shape[0]
    nstate = alog_ref.shape[0]
    spread(mine_ref[:, rank:] + other_ref[:, rank:], wide_s, rows)
    low = (mine_ref[:, :rank] + other_ref[:, :rank]).astype(BF16)
    for group in range(conv_ref.shape[1] // GROUP):
        here = slice(8 * group, 8 * group + 8)
        for sub in range(8):
            at = slice(group * GROUP + sub * LANES, group * GROUP + (sub + 1) * LANES)
            product = jnp.dot(low, dt_ref[:, at], preferred_element_type=F32)
            delta_s[:, sub, :] = softplus(product + bias_ref[:, at])
            x_s[:, sub, :] = conv_ref[:, at].astype(F32)
        fold_rates(alog_ref, rate_s, group)

        def step(block, carry):
            cum, state = carry
            start = block * TOKENS
            ds = [delta_s[start + k] for k in range(TOKENS)]
            xs = [x_s[start + k] for k in range(TOKENS)]
            cums, ys = [], []
            for k in range(TOKENS):
                cum = cum + ds[k]
                dx = ds[k] * xs[k]
                sums = [skip_ref[here, :] * xs[k], jnp.zeros_like(cum)]
                new = []
                for n in range(nstate):
                    row = n * rows + start + k
                    h = jnp.exp2(ds[k] * rate_s[n]) * state[n] + dx * wide_s[pl.ds(row, 1), :]
                    sums[n % 2] = sums[n % 2] + h * wide_s[pl.ds(row + nstate * rows, 1), :]
                    new.append(h)
                state = tuple(new)
                cums.append(cum)
                ys.append(sums[0] + sums[1])
            for k in range(TOKENS):
                cum_ref[start + k, here, :] = cums[k]
                y_ref[start + k, here, :] = ys[k]
            return cum, state

        zero = jnp.zeros((8, LANES), F32)
        cum, state = lax.fori_loop(0, rows // TOKENS, step, (zero, (zero,) * nstate))
        high = cum.astype(BF16).astype(F32)
        message_ref[group] = jnp.concatenate(state + (high, cum - high), axis=0).astype(BF16)


def local_scan(mine, other, dt_proj, dt_bias, a_log, d_skip, conv_out, after):
    rows, channels = conv_out.shape
    nstate = a_log.shape[0]
    subs = channels // LANES
    vmem = pl.BlockSpec(memory_space=pltpu.VMEM)
    return pl.pallas_call(
        scan_kernel,
        in_specs=[vmem] * 7 + [pl.BlockSpec(memory_space=pl.ANY)],
        out_specs=[vmem] * 3,
        out_shape=[
            jax.ShapeDtypeStruct((rows, subs, LANES), F32),
            jax.ShapeDtypeStruct((rows, subs, LANES), F32),
            jax.ShapeDtypeStruct((channels // GROUP, 8 * (nstate + 2), LANES), BF16),
        ],
        scratch_shapes=[
            pltpu.VMEM((rows, 8, LANES), F32),
            pltpu.VMEM((rows, 8, LANES), F32),
            pltpu.VMEM((rows * nstate * 2, LANES), F32),
            pltpu.VMEM((nstate, 8, LANES), F32),
        ],
        compiler_params=params(24),
        cost_estimate=cost(rows * channels * nstate * 1600, rows * channels * 12, rows * channels * nstate),
        name="local_scan",
    )(
        mine, other, dt_proj, dt_bias.reshape(1, channels), a_log, d_skip.reshape(subs, LANES),
        conv_out, after,
    )


def finish_kernel(y_ref, cum_ref, mine_ref, other_ref, state_ref, alog_ref, gate_ref, out_ref, y_s, wide_s, rate_s):
    rows = y_ref.shape[0]
    nstate = alog_ref.shape[0]
    spot = mine_ref.shape[1] - nstate
    spread(mine_ref[:, spot:] + other_ref[:, spot:], wide_s, rows)
    for group in range(gate_ref.shape[1] // GROUP):
        here = slice(8 * group, 8 * group + 8)
        fold_rates(alog_ref, rate_s, group)

        def step(block, carry):
            start = block * TOKENS
            cums = [cum_ref[start + k, here, :] for k in range(TOKENS)]
            ys = [[y_ref[start + k, here, :], jnp.zeros((8, LANES), F32)] for k in range(TOKENS)]
            for n in range(nstate):
                rate, state = rate_s[n], state_ref[group, 8 * n : 8 * n + 8, :]
                for k in range(TOKENS):
                    term = (jnp.exp2(cums[k] * rate) * state) * wide_s[pl.ds(n * rows + start + k, 1), :]
                    ys[k][n % 2] = ys[k][n % 2] + term
            for k in range(TOKENS):
                y_s[start + k] = ys[k][0] + ys[k][1]
            return carry

        lax.fori_loop(0, rows // TOKENS, step, 0)
        for sub in range(8):
            at = slice(group * GROUP + sub * LANES, group * GROUP + (sub + 1) * LANES)
            half = 0.5 * gate_ref[:, at].astype(F32)
            out_ref[:, at] = (y_s[:, sub, :] * (half * jnp.tanh(half) + half)).astype(BF16)


def finish(y, cum, mine, other, incoming, a_log, mamba_gate):
    rows, channels = mamba_gate.shape
    nstate = a_log.shape[0]
    vmem = pl.BlockSpec(memory_space=pltpu.VMEM)
    return pl.pallas_call(
        finish_kernel,
        in_specs=[vmem] * 7,
        out_specs=vmem,
        out_shape=jax.ShapeDtypeStruct((rows, channels), BF16),
        scratch_shapes=[
            pltpu.VMEM((rows, 8, LANES), F32),
            pltpu.VMEM((rows * nstate, LANES), F32),
            pltpu.VMEM((nstate, 8, LANES), F32),
        ],
        compiler_params=params(24),
        cost_estimate=cost(rows * channels * nstate * 1000, rows * channels * 12, rows * channels * nstate),
        name="finish",
    )(y, cum, mine, other, incoming, a_log, mamba_gate)


def join_kernel(size, first, last, place_ref, alog_ref, *refs):
    came, rate_s, refs = refs[:size], refs[-1], refs[size:-1]
    if not first:
        old_sum_ref, old_ref, refs = refs[0], refs[1], refs[2:]
    nstate = alog_ref.shape[0]
    mine = place_ref[0]
    groups = came[0].shape[0]
    for g in range(groups):
        fold_rates(alog_ref, rate_s, g)
        ordered = []
        for j in range(size):
            pick = mine ^ j
            chosen = came[0][g]
            for k in range(1, size):
                chosen = jnp.where(pick == k, came[k][g], chosen)
            ordered.append(chosen.astype(F32))
        row = lambda j, n: ordered[j][8 * n : 8 * n + 8, :]
        added = [row(j, nstate) + row(j, nstate + 1) for j in range(size)]
        zero = jnp.zeros((8, LANES), F32)
        running, prefix = added[0], zero
        for j in range(1, size):
            prefix = jnp.where(mine == j, running, prefix)
            running = running + added[j]
        total_rows = []
        for n in range(nstate):
            rate = rate_s[n]
            state, before = row(0, n), zero
            for j in range(1, size):
                before = jnp.where(mine == j, state, before)
                if j < size - 1 or not last:
                    state = state * jnp.exp2(rate * added[j]) + row(j, n)
            if not first:
                before = before * jnp.exp2(rate * old_sum_ref[g]) + old_ref[g, 8 * n : 8 * n + 8, :]
            refs[0][g, 8 * n : 8 * n + 8, :] = before
            total_rows.append(state)
        if not last:
            refs[1][g] = prefix if first else prefix + old_sum_ref[g]
            high = running.astype(BF16).astype(F32)
            refs[2][g] = jnp.concatenate(total_rows + [high, running - high], axis=0).astype(BF16)


def joined(message, a_log, beside):
    nstate = a_log.shape[0]
    groups = message.shape[0]
    place = lax.axis_index("seq")
    count = lax.axis_size("seq")
    smem = pl.BlockSpec(memory_space=pltpu.SMEM)
    vmem = pl.BlockSpec(memory_space=pltpu.VMEM)
    stride = 1
    old = []
    results = []
    sizes = (4, 2, 4, 4)
    for stage, (size, work) in enumerate(zip(sizes, beside)):
        first, last = stage == 0, stage == len(sizes) - 1
        mine = ((place // stride) % size).astype(jnp.int32).reshape(1)
        came = [message]
        for k in range(1, size):
            pairs = [(i, i ^ (k * stride)) for i in range(count)]
            came.append(lax.ppermute(message, "seq", pairs))
        done = []
        for spot, piece in enumerate(work):
            done.append(piece(done[-1] if spot else came[1] if len(work) > 1 else message))
        if done:
            came, done = lax.optimization_barrier((came, done))
        results.extend(done)
        shapes = [jax.ShapeDtypeStruct((groups, 8 * nstate, LANES), F32)]
        if not last:
            shapes += [jax.ShapeDtypeStruct((groups, 8, LANES), F32), jax.ShapeDtypeStruct(message.shape, BF16)]
        outs = pl.pallas_call(
            functools.partial(join_kernel, size, first, last),
            in_specs=[smem] + [vmem] * (1 + size + len(old)),
            out_specs=[vmem] * len(shapes),
            out_shape=shapes,
            scratch_shapes=[pltpu.VMEM((nstate, 8, LANES), F32)],
            compiler_params=params(16),
            cost_estimate=cost(1e8, message.size * 2 * size, message.size * size),
            name="join",
        )(mine, a_log, *came, *old)
        if not last:
            old = [outs[1], outs[0]]
            message = outs[2]
        stride *= size
    return outs[0], results


def payload_kernel(turn_ref, own_ref, z1_ref, z2_ref, *outs):
    for step, out_ref in enumerate(outs, 1):
        out_ref[0] = z1_ref[...]
        wraps = turn_ref[0] + step >= 4

        @pl.when(wraps)
        def _():
            out_ref[1] = z2_ref[...]

        @pl.when(jnp.logical_not(wraps))
        def _():
            out_ref[1] = own_ref[...]


def payloads(turn, own, z1, z2):
    smem = pl.BlockSpec(memory_space=pltpu.SMEM)
    vmem = pl.BlockSpec(memory_space=pltpu.VMEM)
    return pl.pallas_call(
        payload_kernel,
        in_specs=[smem, vmem, vmem, vmem],
        out_specs=[vmem] * 3,
        out_shape=[jax.ShapeDtypeStruct((2,) + own.shape, BF16)] * 3,
        compiler_params=params(16),
        cost_estimate=cost(0, own.size * 18, 0),
        name="payload",
    )(turn, own, z1, z2)


def prepare_kernel(first_ref, turn_ref, own_ref, z1_ref, z2_ref, r1_ref, r2_ref, r3_ref, key_ref, value_ref):
    rows = own_ref.shape[1]
    local_kv = own_ref.shape[0] // (2 * HEAD_DIM)
    tiles = WINDOW // rows + 1
    first = first_ref[0]
    turn = turn_ref[0]
    pad = LANES - HEAD_DIM
    line = lax.broadcasted_iota(jnp.int32, (pad, rows), 0)
    empty = jnp.zeros((rows, pad), BF16)
    moved = (None, r1_ref, r2_ref, r3_ref)
    for tile in range(tiles):
        at = slice(tile * rows, (tile + 1) * rows)
        if tile % 4 == 0:
            block = (z2_ref, z1_ref, own_ref)[tile // 4][...]
        else:
            step = 4 - tile % 4
            early = tile < 4
            block = moved[step][jnp.where((turn < step) == early, 1, 0)]
        extra = jnp.where(line == 0, jnp.where(tile < first, LOW, 0.0), 0.0).astype(BF16)
        for head in range(local_kv):
            key = block[head * HEAD_DIM : (head + 1) * HEAD_DIM, :]
            value = block[(local_kv + head) * HEAD_DIM : (local_kv + head + 1) * HEAD_DIM, :]
            key_ref[head, :, at] = jnp.concatenate((key, extra), axis=0)
            turned = jnp.transpose(value.astype(F32)).astype(BF16)
            value_ref[head, at, :] = jnp.concatenate((turned, empty), axis=1)


def prepare(first, turn, own, z1, z2, moved):
    rows = own.shape[1]
    local_kv = own.shape[0] // (2 * HEAD_DIM)
    span = WINDOW + rows
    smem = pl.BlockSpec(memory_space=pltpu.SMEM)
    vmem = pl.BlockSpec(memory_space=pltpu.VMEM)
    return pl.pallas_call(
        prepare_kernel,
        in_specs=[smem, smem] + [vmem] * 6,
        out_specs=[vmem, vmem],
        out_shape=[
            jax.ShapeDtypeStruct((local_kv, LANES, span), BF16),
            jax.ShapeDtypeStruct((local_kv, span, LANES), BF16),
        ],
        compiler_params=params(16),
        cost_estimate=cost(1e9, own.size * 18, 0),
        name="prepare",
    )(first, turn, own, z1, z2, *moved)


def attention_kernel(q_ref, key_ref, value_ref, after_ref, *refs):
    earlier, (out_ref, score_a, score_b) = refs[:-3], refs[-3:]
    rows, width = q_ref.shape
    span = key_ref.shape[2]
    tiles = span // rows
    heads = width // HEAD_DIM
    lane = lax.broadcasted_iota(jnp.int32, (rows, LANES - HEAD_DIM), 1)
    one = jnp.where(lane == 0, 1.0, 0.0).astype(BF16)
    qpos = lax.broadcasted_iota(jnp.int32, (rows, rows), 0)
    cpos = lax.broadcasted_iota(jnp.int32, (rows, rows), 1)
    factor = HEAD_DIM ** (-0.5) * LOG2E
    store = (score_a, score_b)

    base = sum(ref.shape[1] for ref in earlier)
    spot = 0
    for ref in earlier:
        out_ref[:, spot : spot + ref.shape[1]] = ref[...]
        spot += ref.shape[1]

    def query_of(head):
        return jnp.concatenate((q_ref[:, head * HEAD_DIM : (head + 1) * HEAD_DIM], one), axis=1)

    def scored(query, head, tile, top):
        at = slice(tile * rows, (tile + 1) * rows)
        score = jnp.dot(query, key_ref[0, :, at], preferred_element_type=F32)
        if tile == 0:
            score = jnp.where(cpos > qpos, score, -jnp.inf)
        if tile == tiles - 1:
            score = jnp.where(cpos <= qpos, score, -jnp.inf)
        store[head % 2][:, at] = score
        for piece in range(rows // LANES):
            top = jnp.maximum(top, score[:, piece * LANES : (piece + 1) * LANES])
        return top

    low = jnp.full((rows, LANES), -jnp.inf, F32)
    top = low
    query = query_of(0)
    for tile in range(tiles):
        top = scored(query, 0, tile, top)
    for head in range(heads):
        best = jnp.max(top, axis=1, keepdims=True)
        total = jnp.zeros((rows, LANES), F32)
        mixed = jnp.zeros((rows, LANES), F32)
        top = low
        if head + 1 < heads:
            query = query_of(head + 1)
        for tile in range(tiles):
            at = slice(tile * rows, (tile + 1) * rows)
            if head + 1 < heads:
                top = scored(query, head + 1, tile, top)
            prob = jnp.exp2((store[head % 2][:, at] - best) * factor)
            for piece in range(rows // LANES):
                total = total + prob[:, piece * LANES : (piece + 1) * LANES]
            mixed = mixed + jnp.dot(prob.astype(BF16), value_ref[0, at, :], preferred_element_type=F32)
        result = mixed / jnp.sum(total, axis=1, keepdims=True)
        at = slice(base + head * HEAD_DIM, base + (head + 1) * HEAD_DIM)
        out_ref[:, at] = result[:, :HEAD_DIM].astype(BF16)


def attention_piece(queries, key, value, piece, after, earlier):
    rows = queries.shape[0]
    local_kv, _, span = key.shape
    heads = queries.shape[1] // HEAD_DIM
    share = heads // PIECES
    kv = piece * share // (heads // local_kv)
    pairs = rows * span * share
    width = share * HEAD_DIM * (1 + len(earlier))
    return pl.pallas_call(
        attention_kernel,
        grid=(1,),
        in_specs=[
            pl.BlockSpec((rows, share * HEAD_DIM), lambda i: (0, piece)),
            pl.BlockSpec((1, LANES, span), lambda i: (kv, 0, 0)),
            pl.BlockSpec((1, span, LANES), lambda i: (kv, 0, 0)),
            pl.BlockSpec(memory_space=pl.ANY),
        ]
        + [pl.BlockSpec((rows, share * HEAD_DIM), lambda i: (0, 0))] * len(earlier),
        out_specs=pl.BlockSpec((rows, width), lambda i: (0, 0)),
        out_shape=jax.ShapeDtypeStruct((rows, width), BF16),
        scratch_shapes=[pltpu.VMEM((rows, span), F32), pltpu.VMEM((rows, span), F32)],
        compiler_params=params(16),
        cost_estimate=cost(pairs * 2600, rows * 4096, pairs),
        name="attention",
    )(queries, key, value, after, *earlier)


def local(
    mamba_in, mamba_gate, conv_weight, conv_bias, x_proj, dt_proj, dt_bias, a_log, d_skip,
    queries, keys, att_values, logits, targets, allowed,
):
    rows, channels = mamba_in.shape
    taps = conv_weight.shape[0]
    nstate = a_log.shape[0]
    subs = channels // LANES
    place = lax.axis_index("seq")
    count = lax.axis_size("seq")
    rim = shifted(mamba_in[rows - (taps - 1) :], "seq", 1)
    own = jnp.concatenate((keys.T, att_values.T), axis=0)
    z1 = shifted(own, "seq", 4)
    z2 = shifted(own, "seq", 8)
    first = jnp.maximum(WINDOW // rows - place, 0).astype(jnp.int32).reshape(1)
    turn = (place % 4).astype(jnp.int32).reshape(1)
    sent = payloads(turn, own, z1, z2)
    moved = []
    for step, payload in enumerate(sent, 1):
        pairs = [(i, i - i % 4 + (i + step) % 4) for i in range(count)]
        moved.append(lax.ppermute(payload, "seq", pairs))
    conv_out, part = convolve(mamba_in, rim, conv_weight, conv_bias, x_proj.T)
    other = swapped(part)
    y, cum, message = local_scan(part, other, dt_proj, dt_bias, a_log, d_skip, conv_out, sent[2])
    made = {}

    def score(message):
        return scoring_part(logits, targets, allowed, [message] + moved)

    def attend(piece):
        def run(message):
            if not made:
                made["kv"] = prepare(first, turn, own, z1, z2, moved)
            pieces = made.setdefault("out", [])
            earlier = pieces if piece == PIECES - 1 else []
            pieces.append(attention_piece(queries, *made["kv"], piece, message, earlier))
            return pieces[-1]

        return run

    incoming, results = joined(message, a_log, [[score], [attend(0)], [attend(1), attend(2)], [attend(3)]])
    stats = results[0]
    attention_out = results[-1]
    others = swapped(stats)
    loglik = scoring_join(stats, others)
    mamba_out = finish(y, cum, part, other, incoming, a_log, mamba_gate)
    return (mamba_out, attention_out, loglik)


def solution(mesh):
    in_specs = (
        P("seq", "vocab"),
        P("seq", "vocab"),
        P(None, "vocab"),
        P("vocab"),
        P("vocab", None),
        P(None, "vocab"),
        P("vocab"),
        P(None, "vocab"),
        P("vocab"),
        P("seq", "vocab"),
        P("seq", "vocab"),
        P("seq", "vocab"),
        P("seq", "vocab"),
        P("seq"),
        P("seq", "vocab"),
    )
    out_specs = (P("seq", "vocab"), P("seq", "vocab"), P("seq"))
    return jax.shard_map(local, mesh=mesh, in_specs=in_specs, out_specs=out_specs, check_vma=False)
```
